32 devices in a mesh: group: 2 (over y), adapter: 4 (over z), tensor: 4 (over x, core).
Axes of the slice: x: 2, y: 2, z: 4, core: 2. Of those that a mesh axis runs over, the one named last changes fastest.
Arguments:
- queries: bfloat16 [1024, 8192], P(('group', 'adapter'), 'tensor'), parts along dimension 0, may hold values from -100 to 100
- cached_key_rows: bfloat16 [1024, 64, 1024], P(('group', 'adapter'), None, 'tensor'), parts along dimension 0, may hold values from -4 to 4
- cached_value_rows: bfloat16 [1024, 64, 1024], P(('group', 'adapter'), None, 'tensor'), parts along dimension 0, may hold values from -4 to 4
- cached_row_length: int32 [1024], P(('group', 'adapter')), parts along dimension 0, may hold values from 2 to 64, as said below
- row_adapter_index: int32 [1024, 1], P(('group', 'adapter')), parts along dimension 0, may hold values from 0 to 3; in each aligned block of 32 rows (0 to 31, 32 to 63, ...) at most 16 rows name the same one
- adapter_slot_index: int32 [8], P('group'), parts along dimension 0, may hold values from 0 to 3, each once
- output_weight: bfloat16 [8192, 8192], P('tensor', 'adapter'), may hold values from -0.0625 to 0.0625
- adapter_down_weight: bfloat16 [8, 8192, 64], P(('group', 'adapter'), 'tensor'), parts along dimension 0, may hold values from -0.0625 to 0.0625
- adapter_up_weight: bfloat16 [8, 64, 8192], P(('group', 'adapter')), parts along dimension 0, may hold values from -0.75 to 0.75
Outputs:
- projected: bfloat16 [1024, 8192], P(('group', 'adapter', 'tensor')), parts along dimension 0
The draws below stay inside these ranges and needn't reach their ends.
There are 2 independent parts, one for each index of `group`. The reference program is written for one: setup_inputs(seed, part) draws one part's arguments, and reference() takes and returns one part's arrays. A program takes and returns all parts, laid end to end along the dimension named above; an argument that names none is the same for every part. Nothing has to cross between parts.
Inputs may be any that keep to these rules, and one draw needn't show every extreme that they name: `cached_row_length`: each row's number of cached positions; some row has all 64. `row_adapter_index`: within each aligned block of 32 rows no adapter is named more than 16 times, and in some block one adapter is named exactly 16 times. A permutation: adapter a is stored at entry adapter_slot_index[a] of adapter_down_weight and adapter_up_weight.
All inputs are finite; a program needn't handle non-finite values.
Results may differ from the reference program's by a relative error of at most 0.013.
Values may be sent and summed in bfloat16 or wider, within the bound.
A program may use at most 128 MiB of HBM per device.

```python
import math
import jax
import jax.numpy as jnp
import numpy as np
from jax import lax

MODEL_DIM = 8192
QUERY_HEAD_COUNT = 64
KV_HEADS = 8
HEAD_WIDTH = 128
ADAPTER_RANK = 64
CTX = 64
ROW_DEV = 32
ROWS = 512
ADAPTER_SLOTS = 4
CAP = 16


def shared_keys(key):
    return jnp.clip(jax.random.normal(key, (ROWS, CTX, KV_HEADS * HEAD_WIDTH), jnp.float32), -4.0, 4.0)


def draw_cached_key_rows(key, part):
    base_keys = shared_keys(key)
    return base_keys.astype(jnp.bfloat16)


def draw_queries(key, part):
    key = jax.random.fold_in(key, 7)
    drawn_queries = jnp.clip(jax.random.normal(key, (ROWS, QUERY_HEAD_COUNT * HEAD_WIDTH), jnp.float32), -4.0, 4.0)
    return drawn_queries.astype(jnp.bfloat16)


def draw_cached_row_length(key, part):
    key = jax.random.fold_in(key, 5)
    drawn_lengths = jax.random.randint(key, (ROWS,), 2, CTX + 1, dtype=jnp.int32)
    return drawn_lengths.at[0].set(CTX)


def levels(own_key, shape, cuts, smallest, largest):
    def one(dim, shards_of):
        draws = jax.random.uniform(jax.random.fold_in(jax.random.fold_in(own_key, 6), dim), (shards_of,), jnp.float32, smallest / len(cuts), largest / len(cuts))
        return jnp.repeat(jnp.exp(draws), shape[dim] // shards_of).reshape((-1,) + (1,) * (len(shape) - dim - 1))

    gain = one(*cuts[0])
    for cut in cuts[1:]:
        gain = gain * one(*cut)
    return gain


def assign_block(key, own, number, rows, amount, top, bound, lean):
    sequence = jax.random.permutation(key, amount)
    crowded, common = shares(amount, rows * top, bound, lean, True), shares(amount, rows * top, bound, lean, False)
    places = jnp.arange(amount)

    def named(lengths, turn):
        used = int((lengths > 0).sum())
        fixed = max(1, used // 4)
        shifted = fixed + (places - fixed + turn * (used - fixed)) % max(1, amount - fixed)
        return jnp.zeros((amount,), jnp.int32).at[sequence[jnp.where(places < fixed, places, shifted)]].set(jnp.asarray(lengths, jnp.int32))

    lengths = jnp.where(number % 4 == 0, named(crowded, number // 4), named(common, number - number // 4 - 1))
    mixed = jax.random.permutation(jax.random.fold_in(own, 3), amount)
    giver, sink = mixed[0:amount // 2 * 2:2], mixed[1:amount // 2 * 2:2]
    margin = jnp.minimum(lengths[giver] - 1, bound - lengths[sink]) // 2
    margin = jnp.where((giver == sequence[0]) | (sink == sequence[0]) | (lengths[sink] == 0), 0, jnp.maximum(margin, 0))
    shifted = jax.random.randint(jax.random.fold_in(own, 4), (amount // 2,), 0, 1 << 20) % (margin + 1)
    lengths = lengths.at[giver].add(-shifted).at[sink].add(shifted)
    labels = jnp.searchsorted(jnp.cumsum(lengths), jnp.arange(rows * top), side="right").astype(jnp.int32)
    listing = labels.reshape(top, rows).T
    listing = listing[jax.random.permutation(jax.random.fold_in(own, 1), rows)]
    turn = jax.random.randint(jax.random.fold_in(own, 2), (rows, 1), 0, top)
    return jnp.take_along_axis(listing, (jnp.arange(top)[None, :] + turn) % top, axis=1)


def shares(number_of, total, bound, slope, full):
    weights = [(1 << 20) // math.isqrt(grade ** slope) + 1 for grade in range(1, number_of + 1)]
    largest = bound if full else min(bound, max(-(-total // number_of), total * weights[0] // sum(weights)))
    least = 1 if total - largest >= number_of - 1 else 0
    counts, spare = [largest] + [least] * (number_of - 1), total - largest - least * (number_of - 1)
    while spare > 0:
        candidates = [i for i in range(1, number_of) if counts[i] < largest] or [i for i in range(1, number_of) if counts[i] < bound]
        pool, remaining = sum([weights[i] for i in candidates]), spare
        for i in candidates:
            extra = min(bound - counts[i], max(1, remaining * weights[i] // pool), spare)
            counts[i] = counts[i] + extra
            spare = spare - extra
    return np.array(counts)


def scatter_about(rng, shape, deviation, most, shards=(), held_as=jnp.bfloat16):
    loudness = levels(rng, shape, shards, -0.22, 0.18) if shards else 1.0
    entries = jax.random.normal(rng, shape, jnp.float32) * deviation * loudness
    return jnp.minimum(jnp.maximum(entries, -most), most).astype(held_as)


def setup_inputs(seed: int = 0, part: int = 0) -> dict:
    key_list = jax.random.split(jax.random.key(seed), 10)
    part_keys = jax.random.split(jax.random.fold_in(key_list[9], part), 10)
    queries = draw_queries(jax.random.fold_in(jax.random.fold_in(key_list[9], part), 71), part)
    cached_key_rows = draw_cached_key_rows(jax.random.fold_in(jax.random.fold_in(key_list[9], part), 71), part)
    cached_value_rows = scatter_about(part_keys[2], (ROWS, CTX, KV_HEADS * HEAD_WIDTH), 1.0, 4.0, ((0, 4), (2, 4)))
    cached_row_length = draw_cached_row_length(jax.random.fold_in(jax.random.fold_in(key_list[9], part), 71), part)
    row_adapter_index_keys = jax.random.split(jax.random.fold_in(part_keys[4], 1), ROWS // ROW_DEV)
    row_adapter_index_turns = jax.random.permutation(jax.random.fold_in(part_keys[4], 3), ROWS // ROW_DEV)
    row_adapter_index = jax.vmap(lambda own, number: assign_block(jax.random.fold_in(part_keys[4], 2), own, number, ROW_DEV, ADAPTER_SLOTS, 1, CAP, 2))(row_adapter_index_keys, row_adapter_index_turns).reshape((ROWS, 1))
    adapter_slot_index = jax.random.permutation(part_keys[5], ADAPTER_SLOTS).astype(jnp.int32)
    output_weight = scatter_about(key_list[6], (QUERY_HEAD_COUNT * HEAD_WIDTH, MODEL_DIM), (QUERY_HEAD_COUNT * HEAD_WIDTH) ** -0.5, 0.0625, ((0, 4), (1, 4)))
    adapter_down_weight = scatter_about(part_keys[7], (ADAPTER_SLOTS, QUERY_HEAD_COUNT * HEAD_WIDTH, ADAPTER_RANK), (QUERY_HEAD_COUNT * HEAD_WIDTH) ** -0.5, 0.0625, ((0, 4), (1, 4)))
    adapter_up_weight = scatter_about(part_keys[8], (ADAPTER_SLOTS, ADAPTER_RANK, MODEL_DIM), ADAPTER_RANK ** -0.5, 0.75, ((0, 4),))
    return dict(queries=queries, cached_key_rows=cached_key_rows, cached_value_rows=cached_value_rows, cached_row_length=cached_row_length, row_adapter_index=row_adapter_index, adapter_slot_index=adapter_slot_index, output_weight=output_weight, adapter_down_weight=adapter_down_weight, adapter_up_weight=adapter_up_weight)


def attend(query_block, key_block, value_block, length_block):
    block_rows = query_block.shape[0]
    group_size = QUERY_HEAD_COUNT // KV_HEADS
    query_heads = query_block.astype(jnp.float32).reshape(block_rows, KV_HEADS, group_size, HEAD_WIDTH)
    cached_keys = key_block.astype(jnp.float32).reshape(block_rows, CTX, KV_HEADS, HEAD_WIDTH)
    cached_values = value_block.astype(jnp.float32).reshape(block_rows, CTX, KV_HEADS, HEAD_WIDTH)
    logits = jnp.einsum("rgsd,rcgd->rgsc", query_heads, cached_keys) * (HEAD_WIDTH ** -0.5)
    visible = (jnp.arange(CTX, dtype=jnp.int32)[None, :] < length_block[:, None])[:, None, None, :]
    logits = jnp.where(visible, logits, -1e30)
    highest = jnp.max(logits, axis=-1, keepdims=True)
    weights = jnp.exp(logits - highest)
    attention_probs = (weights / jnp.sum(weights, axis=-1, keepdims=True)).astype(jnp.bfloat16)
    mixed = jnp.einsum("rgsc,rcgd->rgsd", attention_probs.astype(jnp.float32), cached_values)
    return mixed.astype(jnp.bfloat16).reshape(block_rows, QUERY_HEAD_COUNT * HEAD_WIDTH)


def apply_adapter(attention_block, storage_slot_block, adapter_down_weight, adapter_up_weight):
    down_weight_rows = adapter_down_weight[storage_slot_block].astype(jnp.float32)
    rank_activation = jnp.einsum("bf,bfk->bk", attention_block.astype(jnp.float32), down_weight_rows).astype(jnp.bfloat16)
    up_weight_rows = adapter_up_weight[storage_slot_block].astype(jnp.float32)
    return jnp.einsum("oy,oyx->ox", rank_activation.astype(jnp.float32), up_weight_rows)


def reference(queries, cached_key_rows, cached_value_rows, cached_row_length, row_adapter_index, adapter_slot_index, output_weight, adapter_down_weight, adapter_up_weight):
    block_size = math.gcd(ROWS, 128)
    blocks = ROWS // block_size
    attended = lax.map(
        lambda operand_list: attend(operand_list[0], operand_list[1], operand_list[2], operand_list[3]),
        (queries.reshape(blocks, block_size, QUERY_HEAD_COUNT * HEAD_WIDTH),
         cached_key_rows.reshape(blocks, block_size, CTX, KV_HEADS * HEAD_WIDTH),
         cached_value_rows.reshape(blocks, block_size, CTX, KV_HEADS * HEAD_WIDTH),
         cached_row_length.reshape(blocks, block_size))).reshape(ROWS, QUERY_HEAD_COUNT * HEAD_WIDTH)
    slot_index = adapter_slot_index[row_adapter_index[:, 0]].astype(jnp.int32)
    adapter_update = lax.map(
        lambda operand_list: apply_adapter(operand_list[0], operand_list[1], adapter_down_weight, adapter_up_weight),
        (attended.reshape(blocks, block_size, QUERY_HEAD_COUNT * HEAD_WIDTH),
         slot_index.reshape(blocks, block_size))).reshape(ROWS, MODEL_DIM)
    base_output = jnp.dot(attended, output_weight, preferred_element_type=jnp.float32)
    return (base_output + 2.0 * adapter_update).astype(jnp.bfloat16)
```

```python
import functools

import jax
import jax.numpy as jnp
from jax import lax
from jax.experimental import pallas as pl
from jax.experimental.pallas import tpu as pltpu
from jax.sharding import PartitionSpec as P

HEAD_WIDTH = 128
CHUNKS = 2
PIECE = 16


def remote(src, dst, send, recv, axis, index):
    return pltpu.make_async_remote_copy(
        src_ref=src,
        dst_ref=dst,
        send_sem=send,
        recv_sem=recv,
        device_id={axis: index},
        device_id_type=pl.DeviceIdType.MESH,
    )


def mirror(a, s):
    b = a
    bit = 1
    while bit < 4:
        b = b + ((s // bit) % 2) * (bit - 2 * bit * ((a // bit) % 2))
        bit *= 2
    return b


def attend_rows(q16, k_buf, v_buf, lens16, row0, kv_local, group, context):
    qf = q16.astype(jnp.float32)
    lane = lax.broadcasted_iota(jnp.int32, (8 * group, 2 * context), 1)
    row = lax.broadcasted_iota(jnp.int32, (8 * group, 2 * context), 0) % 8
    own_half = (lane // context) == (row % 2)
    place = lane % context
    pair = row // 2
    out = [[None, None] for _ in range(kv_local * group)]
    for half in range(2):
        q8 = qf[half * 8 : half * 8 + 8]
        lens = jnp.concatenate([lens16[half * 8 : half * 8 + 8]] * group, axis=0)
        visible = own_half & (place < lens)
        for g in range(kv_local):
            lanes = slice(g * HEAD_WIDTH, (g + 1) * HEAD_WIDTH)
            qs = jnp.concatenate(
                [
                    q8[:, (g * group + h) * HEAD_WIDTH : (g * group + h + 1) * HEAD_WIDTH]
                    for h in range(group)
                ],
                axis=0,
            ).astype(jnp.bfloat16)
            keys = k_buf[pl.ds(row0 + half * 8, 8), :, lanes].reshape(8 * context, HEAD_WIDTH)
            vals = v_buf[pl.ds(row0 + half * 8, 8), :, lanes].reshape(8 * context, HEAD_WIDTH)
            cross = lax.dot_general(
                qs, keys, (((1,), (1,)), ((), ())), preferred_element_type=jnp.float32
            )
            width = 2 * context
            logits = cross[:, :width]
            for j in range(1, 4):
                logits = jnp.where(pair == j, cross[:, j * width : (j + 1) * width], logits)
            logits = jnp.where(visible, logits * HEAD_WIDTH ** (-0.5), -1e30)
            weights = jnp.exp(logits - jnp.max(logits, axis=1, keepdims=True))
            probs = weights / jnp.sum(weights, axis=1, keepdims=True)
            spread = jnp.concatenate(
                [jnp.where(pair == j, probs, 0.0) for j in range(4)], axis=1
            ).astype(jnp.bfloat16)
            mixed = jnp.dot(spread, vals, preferred_element_type=jnp.float32)
            for h in range(group):
                out[g * group + h][half] = mixed[8 * h : 8 * h + 8]
    return [jnp.concatenate(pair_of, axis=0).astype(jnp.bfloat16) for pair_of in out]


def fused_kernel(
    n,
    tn,
    q_ref,
    k_hbm,
    v_hbm,
    len_ref,
    radp_ref,
    slot_ref,
    w_hbm,
    down_ref,
    up_hbm,
    out_ref,
    k_buf,
    v_buf,
    w_buf,
    gat,
    part,
    got,
    base,
    mids,
    masks,
    ups,
    done,
    kv_sem,
    w_sem,
    gs,
    gr,
    rs,
    rr,
    ms,
    mr,
    ks,
    kr,
    us,
    ur,
    xs,
    xr,
    ol,
    os,
    orr,
):
    a = lax.axis_index("adapter")
    t = lax.axis_index("tensor")
    rows, feat = q_ref.shape
    cols = w_hbm.shape[1]
    rank = down_ref.shape[2]
    context = k_hbm.shape[1]
    kv_local = k_hbm.shape[2] // HEAD_WIDTH
    group = feat // (kv_local * HEAD_WIDTH)
    quarter = rows // tn
    share = rank // tn
    steps = CHUNKS * n

    for c in range(CHUNKS):
        for x in range(tn):
            at = pl.ds(x * quarter + c * PIECE, PIECE)
            pltpu.make_async_copy(k_hbm.at[at], k_buf.at[at], kv_sem.at[0, c, x]).start()
            pltpu.make_async_copy(v_hbm.at[at], v_buf.at[at], kv_sem.at[1, c, x]).start()
    w_copy = pltpu.make_async_copy(w_hbm, w_buf, w_sem)
    w_copy.start()
    own_cols = pl.ds(pl.multiple_of(a * cols, 128), cols)
    up_local = pltpu.make_async_copy(up_hbm.at[0, :, own_cols], ups.at[a], ol)
    up_local.start()

    barrier = pltpu.get_barrier_semaphore()
    for d in range(1, n):
        pl.semaphore_signal(
            barrier, inc=1, device_id={"adapter": (a + d) % n}, device_id_type=pl.DeviceIdType.MESH
        )
    for d in range(1, tn):
        pl.semaphore_signal(
            barrier, inc=1, device_id={"tensor": (t + d) % tn}, device_id_type=pl.DeviceIdType.MESH
        )
    pl.semaphore_wait(barrier, n + tn - 2)

    mine = pl.ds(pl.multiple_of(t * share, share), share)
    up_sends = []
    for d in range(1, n):
        to = (a + d) % n
        up_sends.append(
            remote(
                up_hbm.at[0, mine, pl.ds(pl.multiple_of(to * cols, 128), cols)],
                ups.at[a, mine, :],
                us.at[d - 1],
                ur.at[a],
                "adapter",
                to,
            )
        )
        up_sends[-1].start()
    named = radp_ref[pl.ds(pl.multiple_of(t * quarter, quarter), quarter), :]
    slot = jnp.zeros_like(named)
    for k in range(n):
        slot = slot + jnp.where(named == k, slot_ref[k], 0)
    lane_slot = lax.broadcasted_iota(jnp.int32, (quarter, n * rank), 1) // rank
    hot = jnp.where(lane_slot == slot, 1.0, 0.0).astype(jnp.bfloat16)
    masks[a] = hot.reshape(CHUNKS, PIECE, n * rank)
    mask_sends = []
    for d in range(1, n):
        to = (a + d) % n
        mask_sends.append(
            remote(masks.at[a], masks.at[a], ks.at[d - 1], kr.at[a], "adapter", to)
        )
        mask_sends[-1].start()

    def up_line(b, c):
        return remote(
            gat.at[b, c], gat.at[b, c], gs.at[0, b, c], gr.at[b, c], "adapter", (a + 1) % n
        )

    def down_line(b, c):
        return remote(
            gat.at[b, c], gat.at[b, c], gs.at[1, b, c], gr.at[b, c], "adapter", (a + n - 1) % n
        )

    for c in range(CHUNKS):

        def attend_step(x, carry, c=c):
            row0 = pl.multiple_of(x * quarter + c * PIECE, PIECE)
            at = pl.ds(row0, PIECE)
            pltpu.make_async_copy(k_hbm.at[at], k_buf.at[at], kv_sem.at[0, c, x]).wait()
            pltpu.make_async_copy(v_hbm.at[at], v_buf.at[at], kv_sem.at[1, c, x]).wait()
            heads = attend_rows(
                q_ref[at, :], k_buf, v_buf, len_ref[at, :], row0, kv_local, group, context
            )
            to = pl.ds(pl.multiple_of(x * PIECE, PIECE), PIECE)
            for h, value in enumerate(heads):
                gat[a, c, to, h * HEAD_WIDTH : (h + 1) * HEAD_WIDTH] = value
            return carry

        lax.fori_loop(0, tn, attend_step, 0)

        @pl.when(a < n - 1)
        def _(c=c):
            up_line(a, c).start()

        @pl.when(a > 0)
        def _(c=c):
            down_line(a, c).start()

    share_sends = []
    for d in range(1, n):
        source = (a + d) % n
        remote(ups.at[source, mine, :], ups.at[source, mine, :], us.at[0], ur.at[source],
               "adapter", source).wait_recv()
        for e in range(1, tn):
            share_sends.append(
                remote(
                    ups.at[source, mine, :],
                    ups.at[source, mine, :],
                    xs.at[d - 1, e - 1],
                    xr.at[d - 1, e - 1],
                    "tensor",
                    (t + e) % tn,
                )
            )
            share_sends[-1].start()
    w_copy.wait()

    def scatter(i, e):
        return remote(
            part.at[i, (t + e) % tn], got.at[i, e - 1], rs.at[i, e - 1], rr.at[i, e - 1],
            "tensor", (t + e) % tn,
        )

    def mid_send(c, b, i, d):
        return remote(
            mids.at[c, b, a], mids.at[c, b, a], ms.at[i, d - 1], mr.at[c, b, a],
            "adapter", (a + d) % n,
        )

    def multiply(i):
        c, s = i // n, i % n

        @pl.when((s > 0) & (a - s >= 0))
        def _():
            up_line(a - s, c).wait_recv()

            @pl.when(a < n - 1)
            def _():
                up_line(a - s, c).start()

        @pl.when((s > 0) & (a + s < n))
        def _():
            down_line(a + s, c).wait_recv()

            @pl.when(a > 0)
            def _():
                down_line(a + s, c).start()

        b = mirror(a, s)
        x = gat[b, c]
        tile = 512
        low = jnp.dot(x, down_ref[0], preferred_element_type=jnp.float32)
        low = jnp.concatenate([low, jnp.zeros_like(low)], axis=1).astype(jnp.bfloat16)
        part[i, :, :, cols : cols + 2 * rank] = low.reshape(tn, PIECE, 2 * rank)
        for j in range(cols // tile):
            y = jnp.dot(
                x, w_buf[:, j * tile : (j + 1) * tile], preferred_element_type=jnp.float32
            )
            part[i, :, :, j * tile : (j + 1) * tile] = y.astype(jnp.bfloat16).reshape(
                tn, PIECE, tile
            )
        for e in range(1, tn):
            scatter(i, e).start()

    def add_up(i):
        c, s = i // n, i % n
        b = mirror(a, s)
        for e in range(1, tn):
            scatter(i, e).wait_recv()
        total = part[i, t].astype(jnp.float32)
        for e in range(1, tn):
            total = total + got[i, e - 1].astype(jnp.float32)
        base[i] = total[:, :cols]
        mids[c, b, a] = total[:, cols:].astype(jnp.bfloat16)
        for d in range(1, n):
            mid_send(c, b, i, d).start()

    def result(c, s):
        return remote(
            done.at[c * n + s],
            out_ref.at[pl.ds(pl.multiple_of(c * PIECE, PIECE), PIECE), own_cols],
            os.at[c * n + s],
            orr.at[c, a],
            "adapter",
            mirror(a, s),
        )

    def finish(c, s):
        i = c * n + s
        b = mirror(a, s)
        for d in range(1, n):
            source = (a + d) % n
            remote(mids.at[c, b, source], mids.at[c, b, source], ms.at[0, 0],
                   mr.at[c, b, source], "adapter", source).wait_recv()
        low = jnp.concatenate(
            [mids[c, b, k].astype(jnp.float32)[:, :rank] for k in range(n)], axis=1
        )
        low = jnp.where(masks[b, c].astype(jnp.float32) > 0.5, low, 0.0).astype(jnp.bfloat16)
        delta = jnp.dot(
            low, ups[...].reshape(n * rank, cols), preferred_element_type=jnp.float32
        )
        y = (base[i] + 2.0 * delta).astype(jnp.bfloat16)

        @pl.when(s == 0)
        def _():
            out_ref[pl.ds(pl.multiple_of(c * PIECE, PIECE), PIECE), own_cols] = y

        @pl.when(s > 0)
        def _():
            done[i] = y
            result(c, s).start()

    def step(i, carry):
        @pl.when(i < steps)
        def _():
            multiply(i)

        @pl.when(i > 0)
        def _():
            add_up(i - 1)

        @pl.when(i == n)
        def _():
            up_local.wait()
            for d in range(1, n):
                source = (a + d) % n
                remote(masks.at[source], masks.at[source], ks.at[0], kr.at[source],
                       "adapter", source).wait_recv()
                for e in range(1, tn):
                    other = pl.ds(pl.multiple_of(((t + tn - e) % tn) * share, share), share)
                    remote(ups.at[source, other, :], ups.at[source, other, :],
                           xs.at[0, 0], xr.at[d - 1, e - 1],
                           "tensor", (t + e) % tn).wait_recv()

        @pl.when(i > n)
        def _():
            finish(0, i - n - 1)

        return carry

    lax.fori_loop(0, steps + 1, step, 0)

    def last(s, carry):
        finish(1, s)
        return carry

    lax.fori_loop(0, n, last, 0)

    for c in range(CHUNKS):
        for d in range(1, n):
            source = (a + d) % n
            there = pl.ds(pl.multiple_of(source * cols, 128), cols)
            remote(done.at[0], out_ref.at[pl.ds(c * PIECE, PIECE), there], os.at[0],
                   orr.at[c, source], "adapter", source).wait_recv()
    for copy in up_sends + mask_sends + share_sends:
        copy.wait_send()

    def settle(i, carry):
        c, s = i // n, i % n
        b = mirror(a, s)
        for e in range(1, tn):
            scatter(i, e).wait_send()
        for d in range(1, n):
            mid_send(c, b, i, d).wait_send()

        @pl.when(s > 0)
        def _():
            result(c, s).wait_send()

        @pl.when((s <= a) & (a < n - 1))
        def _():
            up_line(s, c).wait_send()

        @pl.when((s >= a) & (a > 0))
        def _():
            down_line(s, c).wait_send()

        return carry

    lax.fori_loop(0, steps, settle, 0)


def fused(
    queries,
    cached_key_rows,
    cached_value_rows,
    cached_row_length,
    row_adapter_index,
    adapter_slot_index,
    output_weight,
    adapter_down_weight,
    adapter_up_weight,
):
    n, tn = lax.axis_size("adapter"), lax.axis_size("tensor")
    rows, feat = queries.shape
    cols = output_weight.shape[1]
    rank = adapter_down_weight.shape[2]
    steps = CHUNKS * n
    bf16, f32 = jnp.bfloat16, jnp.float32
    dma = pltpu.SemaphoreType.DMA
    vmem = pl.BlockSpec(memory_space=pltpu.VMEM)
    hbm = pl.BlockSpec(memory_space=pl.ANY)
    smem = pl.BlockSpec(memory_space=pltpu.SMEM)
    return pl.pallas_call(
        functools.partial(fused_kernel, n, tn),
        out_shape=jax.ShapeDtypeStruct((rows // tn, n * cols), bf16),
        in_specs=[vmem, hbm, hbm, vmem, vmem, smem, hbm, vmem, hbm],
        out_specs=vmem,
        scratch_shapes=[
            pltpu.VMEM(cached_key_rows.shape, bf16),
            pltpu.VMEM(cached_value_rows.shape, bf16),
            pltpu.VMEM(output_weight.shape, bf16),
            pltpu.VMEM((n, CHUNKS, tn * PIECE, feat), bf16),
            pltpu.VMEM((steps, tn, PIECE, cols + 2 * rank), bf16),
            pltpu.VMEM((steps, tn - 1, PIECE, cols + 2 * rank), bf16),
            pltpu.VMEM((steps, PIECE, cols), f32),
            pltpu.VMEM((CHUNKS, n, n, PIECE, 2 * rank), bf16),
            pltpu.VMEM((n, CHUNKS, PIECE, n * rank), bf16),
            pltpu.VMEM((n, rank, cols), bf16),
            pltpu.VMEM((steps, PIECE, cols), bf16),
            dma((2, CHUNKS, tn)),
            dma,
            dma((2, n, CHUNKS)),
            dma((n, CHUNKS)),
            dma((steps, tn - 1)),
            dma((steps, tn - 1)),
            dma((steps, n - 1)),
            dma((CHUNKS, n, n)),
            dma((n - 1,)),
            dma((n,)),
            dma((n - 1,)),
            dma((n,)),
            dma((n - 1, tn - 1)),
            dma((n - 1, tn - 1)),
            dma,
            dma((steps,)),
            dma((CHUNKS, n)),
        ],
        compiler_params=pltpu.CompilerParams(
            collective_id=0, has_side_effects=True, vmem_limit_bytes=56 * 1024 * 1024
        ),
    )(
        queries,
        cached_key_rows,
        cached_value_rows,
        cached_row_length[:, None],
        row_adapter_index,
        adapter_slot_index,
        output_weight,
        adapter_down_weight,
        adapter_up_weight,
    )


def per_device(
    queries,
    cached_key_rows,
    cached_value_rows,
    cached_row_length,
    row_adapter_index,
    adapter_slot_index,
    output_weight,
    adapter_down_weight,
    adapter_up_weight,
):
    row_count = queries.shape[0]
    tensor_count = lax.axis_size("tensor")
    owner_count = lax.axis_size("adapter")
    quarter_rows = row_count // tensor_count
    capacity = max(2, 2 * quarter_rows // owner_count)
    context = cached_key_rows.shape[1]
    kv_local = cached_key_rows.shape[2] // HEAD_WIDTH
    query_heads = queries.reshape(row_count, kv_local, -1, HEAD_WIDTH)
    cached_keys = cached_key_rows.reshape(row_count, context, kv_local, HEAD_WIDTH)
    cached_values = cached_value_rows.reshape(row_count, context, kv_local, HEAD_WIDTH)
    logits = jnp.einsum(
        "rgsd,rcgd->rgsc", query_heads, cached_keys, preferred_element_type=jnp.float32
    ) * HEAD_WIDTH ** (-0.5)
    visible = (jnp.arange(context, dtype=jnp.int32)[None, :] < cached_row_length[:, None])[
        :, None, None, :
    ]
    logits = jnp.where(visible, logits, -1e30)
    highest = jnp.max(logits, axis=-1, keepdims=True)
    weights = jnp.exp(logits - highest)
    attention_probs = (weights / jnp.sum(weights, axis=-1, keepdims=True)).astype(jnp.bfloat16)
    attended = jnp.einsum(
        "rgsc,rcgd->rgsd", attention_probs, cached_values, preferred_element_type=jnp.float32
    )
    attended = attended.astype(jnp.bfloat16).reshape(row_count, -1)
    row_adapter = row_adapter_index[:, 0]
    adapter_count = adapter_slot_index.shape[0]
    matches = row_adapter[:, None] == jnp.arange(adapter_count, dtype=jnp.int32)[None, :]
    slot_index = jnp.sum(jnp.where(matches, adapter_slot_index[None, :], 0), axis=1)
    owner_hot = (slot_index[:, None] == jnp.arange(owner_count, dtype=jnp.int32)[None, :]).astype(
        jnp.int32
    )
    owner_hot = owner_hot.reshape(tensor_count, quarter_rows, owner_count)
    position = jnp.cumsum(owner_hot, axis=1) - 1
    placing = owner_hot[..., None] * (
        position[..., None] == jnp.arange(capacity, dtype=jnp.int32)
    ).astype(jnp.int32)
    split_heads = attended.reshape(tensor_count, quarter_rows, -1)
    send_rows = jnp.einsum(
        "qrjc,qrf->jqcf",
        placing.astype(jnp.bfloat16),
        split_heads,
        preferred_element_type=jnp.float32,
    ).astype(jnp.bfloat16)
    received_parts = lax.all_to_all(send_rows, "adapter", split_axis=0, concat_axis=0, tiled=True)
    rank_terms = jnp.einsum(
        "pato,ow->patw", received_parts, adapter_down_weight[0], preferred_element_type=jnp.float32
    )
    own_terms = lax.psum_scatter(rank_terms, "tensor", scatter_dimension=1, tiled=True)[:, 0]
    rank_activation = own_terms.astype(jnp.bfloat16)
    adapter_terms = jnp.einsum(
        "yhl,lq->yhq", rank_activation, adapter_up_weight[0], preferred_element_type=jnp.float32
    )
    panels = jnp.dot(
        lax.all_gather(attended, "adapter", axis=0, tiled=True),
        output_weight,
        preferred_element_type=jnp.float32,
    )
    shares = lax.psum_scatter(
        panels.reshape(owner_count, tensor_count, quarter_rows, -1),
        "tensor",
        scatter_dimension=1,
        tiled=True,
    )
    base_output_block, adapter_block = (
        lax.all_to_all(
            shares.reshape(owner_count, quarter_rows, -1),
            "adapter",
            split_axis=0,
            concat_axis=2,
            tiled=True,
        ),
        lax.all_to_all(adapter_terms, "adapter", split_axis=0, concat_axis=2, tiled=True),
    )
    base_output_rows = base_output_block[0]
    returned_result = adapter_block[0]
    model_width = base_output_rows.shape[1]
    gathered_terms = returned_result.reshape(capacity, owner_count, model_width)
    own_place = lax.dynamic_index_in_dim(
        placing, lax.axis_index("tensor"), 0, keepdims=False
    ).astype(jnp.float32)
    adapter_rows = jnp.einsum(
        "rjc,cjd->rd", own_place, gathered_terms, precision=lax.Precision.HIGHEST
    )
    return (base_output_rows + 2.0 * adapter_rows).astype(jnp.bfloat16)


def solution(mesh):
    short_line = mesh.shape["adapter"] == 4 and mesh.shape["tensor"] == 4
    return jax.shard_map(
        fused if short_line else per_device,
        mesh=mesh,
        in_specs=(
            P(("group", "adapter"), "tensor"),
            P(("group", "adapter"), None, "tensor"),
            P(("group", "adapter"), None, "tensor"),
            P(("group", "adapter")),
            P(("group", "adapter"), None),
            P("group"),
            P("tensor", "adapter"),
            P(("group", "adapter"), "tensor", None),
            P(("group", "adapter"), None, None),
        ),
        out_specs=P(("group", "adapter", "tensor"), None),
        check_vma=False,
    )
```

```python
import functools

import jax
import jax.numpy as jnp
from jax import lax
from jax.experimental import pallas as pl
from jax.experimental.pallas import tpu as pltpu
from jax.sharding import PartitionSpec as P

HEAD_WIDTH = 128
CHUNKS = 2
PIECE = 16


def remote(src, dst, send, recv, axis, index):
    return pltpu.make_async_remote_copy(
        src_ref=src,
        dst_ref=dst,
        send_sem=send,
        recv_sem=recv,
        device_id={axis: index},
        device_id_type=pl.DeviceIdType.MESH,
    )


def mirror(a, s):
    b = a
    bit = 1
    while bit < 4:
        b = b + ((s // bit) % 2) * (bit - 2 * bit * ((a // bit) % 2))
        bit *= 2
    return b


def as_columns(row):
    count = row.shape[1]
    own = lax.broadcasted_iota(jnp.int32, (count, count), 0) == lax.broadcasted_iota(
        jnp.int32, (count, count), 1
    )
    line = jnp.where(own, jnp.broadcast_to(row.astype(jnp.float32), (count, count)), 0.0)
    return jnp.broadcast_to(jnp.sum(line, axis=1, keepdims=True), (count, count))


def step_bits(a, c, j):
    left = 3 - j
    inner = (a % 3 + 1) // 2
    return (1 - c) * j + c * (left + inner * (left // 2 - 2 * (left // 3)))


def attend_rows(q16, k_buf, v_buf, lens16, row0, kv_local, group, context):
    qf = q16.astype(jnp.float32)
    lane = lax.broadcasted_iota(jnp.int32, (8 * group, 2 * context), 1)
    row = lax.broadcasted_iota(jnp.int32, (8 * group, 2 * context), 0) % 8
    own_half = (lane // context) == (row % 2)
    place = lane % context
    pair = row // 2
    out = [[None, None] for _ in range(kv_local * group)]
    for half in range(2):
        q8 = qf[half * 8 : half * 8 + 8]
        lens = jnp.concatenate([lens16[half * 8 : half * 8 + 8]] * group, axis=0)
        visible = own_half & (place.astype(jnp.float32) < lens)
        for g in range(kv_local):
            lanes = slice(g * HEAD_WIDTH, (g + 1) * HEAD_WIDTH)
            qs = jnp.concatenate(
                [
                    q8[:, (g * group + h) * HEAD_WIDTH : (g * group + h + 1) * HEAD_WIDTH]
                    for h in range(group)
                ],
                axis=0,
            ).astype(jnp.bfloat16)
            keys = k_buf[pl.ds(row0 + half * 8, 8), :, lanes].reshape(8 * context, HEAD_WIDTH)
            vals = v_buf[pl.ds(row0 + half * 8, 8), :, lanes].reshape(8 * context, HEAD_WIDTH)
            cross = lax.dot_general(
                qs, keys, (((1,), (1,)), ((), ())), preferred_element_type=jnp.float32
            )
            width = 2 * context
            logits = cross[:, :width]
            for j in range(1, 4):
                logits = jnp.where(pair == j, cross[:, j * width : (j + 1) * width], logits)
            logits = jnp.where(visible, logits * HEAD_WIDTH ** (-0.5), -1e30)
            weights = jnp.exp(logits - jnp.max(logits, axis=1, keepdims=True))
            probs = weights / jnp.sum(weights, axis=1, keepdims=True)
            spread = jnp.concatenate(
                [jnp.where(pair == j, probs, 0.0) for j in range(4)], axis=1
            ).astype(jnp.bfloat16)
            mixed = jnp.dot(spread, vals, preferred_element_type=jnp.float32)
            for h in range(group):
                out[g * group + h][half] = mixed[8 * h : 8 * h + 8]
    return [jnp.concatenate(pair_of, axis=0).astype(jnp.bfloat16) for pair_of in out]


def fused_kernel(
    n,
    tn,
    q_ref,
    k_hbm,
    v_hbm,
    len_ref,
    radp_ref,
    slot_ref,
    w_hbm,
    down_ref,
    up_hbm,
    out_ref,
    k_buf,
    v_buf,
    w_buf,
    lens,
    slots,
    gat,
    part,
    got,
    half,
    other,
    base,
    lows,
    low_got,
    mids,
    masks,
    ups,
    done,
    kv_sem,
    w_sem,
    gs,
    gr,
    rs,
    rr,
    ls,
    lr,
    ms,
    mr,
    ks,
    kr,
    us,
    ur,
    xs,
    xr,
    ol,
    os,
    orr,
):
    a = lax.axis_index("adapter")
    t = lax.axis_index("tensor")
    core, chip = t % 2, t // 2
    core_peer, chip_peer = mirror(t, 1), mirror(t, 2)
    rows, feat = q_ref.shape
    cols = w_hbm.shape[1]
    rank = down_ref.shape[1]
    context = k_hbm.shape[1]
    kv_local = k_hbm.shape[2] // HEAD_WIDTH
    group = feat // (kv_local * HEAD_WIDTH)
    quarter = rows // tn
    share = rank // tn
    steps = CHUNKS * n

    for c in range(CHUNKS):
        for x in range(tn):
            at = pl.ds(x * quarter + c * PIECE, PIECE)
            pltpu.make_async_copy(k_hbm.at[at], k_buf.at[at], kv_sem.at[0, c, x]).start()
            pltpu.make_async_copy(v_hbm.at[at], v_buf.at[at], kv_sem.at[1, c, x]).start()
    w_copy = pltpu.make_async_copy(w_hbm, w_buf, w_sem)
    w_copy.start()
    own_cols = pl.ds(pl.multiple_of(a * cols, 128), cols)
    up_local = pltpu.make_async_copy(up_hbm.at[0, :, own_cols], ups.at[a], ol)
    up_local.start()

    barrier = pltpu.get_barrier_semaphore()
    for d in range(1, n):
        pl.semaphore_signal(
            barrier, inc=1, device_id={"adapter": (a + d) % n}, device_id_type=pl.DeviceIdType.MESH
        )
    for d in range(1, tn):
        pl.semaphore_signal(
            barrier, inc=1, device_id={"tensor": (t + d) % tn}, device_id_type=pl.DeviceIdType.MESH
        )
    pl.semaphore_wait(barrier, n + tn - 2)

    mine = pl.ds(pl.multiple_of(t * share, share), share)
    up_sends = []
    for d in range(1, n):
        to = (a + d) % n
        up_sends.append(
            remote(
                up_hbm.at[0, mine, pl.ds(pl.multiple_of(to * cols, 128), cols)],
                ups.at[a, mine, :],
                us.at[d - 1],
                ur.at[a],
                "adapter",
                to,
            )
        )
        up_sends[-1].start()
    lens[...] = as_columns(len_ref[...])
    named = radp_ref[...]
    slot = jnp.zeros_like(named)
    for k in range(n):
        slot = slot + jnp.where(named == k, slot_ref[k], 0)
    slots[...] = as_columns(slot)
    slot = slots[pl.ds(pl.multiple_of(t * quarter, quarter), quarter), :]
    slot = jnp.concatenate([slot] * (n * rank // rows), axis=1)
    lane_slot = lax.broadcasted_iota(jnp.int32, (quarter, n * rank), 1) // rank
    hot = jnp.where(lane_slot.astype(jnp.float32) == slot, 1.0, 0.0).astype(jnp.bfloat16)
    masks[a] = hot.reshape(CHUNKS, PIECE, n * rank)
    mask_sends = []
    for d in range(1, n):
        to = (a + d) % n
        mask_sends.append(
            remote(masks.at[a], masks.at[a], ks.at[d - 1], kr.at[a], "adapter", to)
        )
        mask_sends[-1].start()

    def up_line(b, c):
        return remote(
            gat.at[b, c], gat.at[b, c], gs.at[0, b, c], gr.at[b, c], "adapter", (a + 1) % n
        )

    def down_line(b, c):
        return remote(
            gat.at[b, c], gat.at[b, c], gs.at[1, b, c], gr.at[b, c], "adapter", (a + n - 1) % n
        )

    for c in range(CHUNKS):

        def attend_step(x, carry, c=c):
            row0 = pl.multiple_of(x * quarter + c * PIECE, PIECE)
            at = pl.ds(row0, PIECE)
            pltpu.make_async_copy(k_hbm.at[at], k_buf.at[at], kv_sem.at[0, c, x]).wait()
            pltpu.make_async_copy(v_hbm.at[at], v_buf.at[at], kv_sem.at[1, c, x]).wait()
            heads = attend_rows(
                q_ref[at, :], k_buf, v_buf, lens[at, :], row0, kv_local, group, context
            )
            to = pl.ds(pl.multiple_of(x * PIECE, PIECE), PIECE)
            for h, value in enumerate(heads):
                gat[a, c, to, h * HEAD_WIDTH : (h + 1) * HEAD_WIDTH] = value
            return carry

        lax.fori_loop(0, tn, attend_step, 0)

        if c == 0:

            @pl.when(a < n - 1)
            def _():
                up_line(a, 0).start()

            @pl.when(a > 0)
            def _():
                down_line(a, 0).start()

    w_copy.wait()

    def part_of(index):
        return pl.ds(pl.multiple_of(index * share, share), share)

    def share_copy(d, k):
        source = (a + d) % n
        at = part_of(chip_peer if k == 2 else t)
        return remote(
            ups.at[source, at, :], ups.at[source, at, :], xs.at[d - 1, k], xr.at[d - 1, k],
            "tensor", chip_peer if k == 1 else core_peer,
        )

    def share_wait(d, k):
        source = (a + d) % n
        at = part_of(mirror(t, k + 1))
        remote(
            ups.at[source, at, :], ups.at[source, at, :], xs.at[d - 1, k], xr.at[d - 1, k],
            "tensor", chip_peer if k == 1 else core_peer,
        ).wait_recv()

    def low_send(c, b, e):
        to = mirror(t, e)
        return remote(
            lows.at[c, b, to], low_got.at[c, b, e - 1], ls.at[c, b, e - 1], lr.at[c, b, e - 1],
            "tensor", to,
        )

    def mid_send(c, b, d):
        return remote(
            mids.at[c, b, a], mids.at[c, b, a], ms.at[c, b, d - 1], mr.at[c, b, a],
            "adapter", (a + d) % n,
        )

    def core_send(i):
        return remote(
            part.at[i, 1 - core], got.at[i], rs.at[i, 0], rr.at[i, 0], "tensor", core_peer
        )

    def chip_send(i):
        return remote(half.at[i], other.at[i], rs.at[i, 1], rr.at[i, 1], "tensor", chip_peer)

    def low(c, b):
        y = lax.dot_general(
            gat[b, c], down_ref[0], (((1,), (1,)), ((), ())), preferred_element_type=jnp.float32
        )
        y = jnp.concatenate([y, jnp.zeros_like(y)], axis=1).astype(jnp.bfloat16)
        lows[c, b] = y.reshape(tn, PIECE, 2 * rank)
        for e in range(1, tn):
            low_send(c, b, e).start()

    def mid(c, b):
        total = lows[c, b, t].astype(jnp.float32)
        for e in range(1, tn):
            low_send(c, b, e).wait_recv()
            total = total + low_got[c, b, e - 1].astype(jnp.float32)
        mids[c, b, a] = total.astype(jnp.bfloat16)
        for d in range(1, n):
            mid_send(c, b, d).start()

    def multiply(i):
        c, j = i // n, i % n
        below = (1 - c) * (a - j) + c * j
        above = (1 - c) * (a + j) + c * (n - 1 - j)
        from_below = (below >= 0) & (below < a)
        from_above = (above < n) & (above > a)

        @pl.when(from_above)
        def _():
            down_line(above, c).wait_recv()

            @pl.when(a > 0)
            def _():
                down_line(above, c).start()

        @pl.when((c == 1) & (above == a) & (a > 0))
        def _():
            down_line(a, 1).start()

        @pl.when(from_below)
        def _():
            up_line(below, c).wait_recv()

            @pl.when(a < n - 1)
            def _():
                up_line(below, c).start()

        @pl.when((c == 1) & (below == a) & (a < n - 1))
        def _():
            up_line(a, 1).start()

        @pl.when(from_above)
        def _():
            low(c, above)

        @pl.when(from_below)
        def _():
            low(c, below)

        @pl.when(j == 0)
        def _():
            low(c, a)

        x = gat[mirror(a, step_bits(a, c, j)), c]
        tile = 512
        for k in range(cols // tile):
            lanes = slice(k * tile, (k + 1) * tile)
            y = jnp.dot(x, w_buf[:, lanes], preferred_element_type=jnp.float32)
            y = y.astype(jnp.bfloat16)
            for piece in range(tn):
                part[i, piece % 2, piece // 2, :, lanes] = y[piece * PIECE : (piece + 1) * PIECE]
        core_send(i).start()

        @pl.when(from_above)
        def _():
            mid(c, above)

        @pl.when(from_below)
        def _():
            mid(c, below)

        @pl.when(j == 0)
        def _():
            mid(c, a)

    def pair(i):
        core_send(i).wait_recv()
        away = part[i, core, 1 - chip].astype(jnp.float32) + got[i, 1 - chip].astype(jnp.float32)
        half[i] = away.astype(jnp.bfloat16)
        chip_send(i).start()
        base[i] = part[i, core, chip].astype(jnp.float32) + got[i, chip].astype(jnp.float32)

    def add_up(i):
        chip_send(i).wait_recv()
        base[i] = base[i] + other[i].astype(jnp.float32)

    def result(c, j):
        return remote(
            done.at[c * n + j],
            out_ref.at[pl.ds(pl.multiple_of(c * PIECE, PIECE), PIECE), own_cols],
            os.at[c * n + j],
            orr.at[c, a],
            "adapter",
            mirror(a, step_bits(a, c, j)),
        )

    def finish(c, j):
        i = c * n + j
        s = step_bits(a, c, j)
        b = mirror(a, s)
        for d in range(1, n):
            source = (a + d) % n
            remote(mids.at[c, b, source], mids.at[c, b, source], ms.at[0, 0, 0],
                   mr.at[c, b, source], "adapter", source).wait_recv()
        low = jnp.concatenate(
            [mids[c, b, k].astype(jnp.float32)[:, :rank] for k in range(n)], axis=1
        )
        low = jnp.where(masks[b, c].astype(jnp.float32) > 0.5, low, 0.0).astype(jnp.bfloat16)
        delta = jnp.dot(
            low, ups[...].reshape(n * rank, cols), preferred_element_type=jnp.float32
        )
        y = (base[i] + 2.0 * delta).astype(jnp.bfloat16)

        @pl.when(s == 0)
        def _():
            out_ref[pl.ds(pl.multiple_of(c * PIECE, PIECE), PIECE), own_cols] = y

        @pl.when(s > 0)
        def _():
            done[i] = y
            result(c, j).start()

    def step(i, carry):
        @pl.when(i < steps)
        def _():
            multiply(i)

        @pl.when(i == 1)
        def _():
            for d in range(1, n):
                source = (a + d) % n
                remote(ups.at[source, mine, :], ups.at[source, mine, :], us.at[0], ur.at[source],
                       "adapter", source).wait_recv()
                share_copy(d, 0).start()
                share_copy(d, 1).start()

        @pl.when(i == 2)
        def _():
            for d in range(1, n):
                share_wait(d, 1)
                share_copy(d, 2).start()

        @pl.when((i > 0) & (i <= steps))
        def _():
            pair(i - 1)

        @pl.when(i > 1)
        def _():
            add_up(i - 2)

        @pl.when(i == n)
        def _():
            up_local.wait()
            for d in range(1, n):
                source = (a + d) % n
                remote(masks.at[source], masks.at[source], ks.at[0], kr.at[source],
                       "adapter", source).wait_recv()
                share_wait(d, 0)
                share_wait(d, 2)

        @pl.when((i == n + 1) | (i == n + 2))
        def _():
            def early(k, inner):
                finish(0, (i - n - 1) * 2 + k)
                return inner

            lax.fori_loop(0, 2, early, 0)

        @pl.when(i >= n + 2)
        def _():
            finish(1, i - n - 2)

        return carry

    lax.fori_loop(0, steps + 2, step, 0)

    for c in range(CHUNKS):
        for d in range(1, n):
            source = (a + d) % n
            there = pl.ds(pl.multiple_of(source * cols, 128), cols)
            remote(done.at[0], out_ref.at[pl.ds(c * PIECE, PIECE), there], os.at[0],
                   orr.at[c, source], "adapter", source).wait_recv()
    for copy in up_sends + mask_sends:
        copy.wait_send()
    for d in range(1, n):
        for k in range(3):
            share_copy(d, k).wait_send()

    def settle(i, carry):
        c, s = i // n, i % n
        core_send(i).wait_send()
        chip_send(i).wait_send()
        for e in range(1, tn):
            low_send(c, s, e).wait_send()
        for d in range(1, n):
            mid_send(c, s, d).wait_send()

        @pl.when(step_bits(a, c, s) > 0)
        def _():
            result(c, s).wait_send()

        @pl.when((s <= a) & (a < n - 1))
        def _():
            up_line(s, c).wait_send()

        @pl.when((s >= a) & (a > 0))
        def _():
            down_line(s, c).wait_send()

        return carry

    lax.fori_loop(0, steps, settle, 0)


def fused(
    queries,
    cached_key_rows,
    cached_value_rows,
    cached_row_length,
    row_adapter_index,
    adapter_slot_index,
    output_weight,
    adapter_down_weight,
    adapter_up_weight,
):
    n, tn = lax.axis_size("adapter"), lax.axis_size("tensor")
    rows, feat = queries.shape
    cols = output_weight.shape[1]
    rank = adapter_down_weight.shape[2]
    steps = CHUNKS * n
    bf16, f32 = jnp.bfloat16, jnp.float32
    dma = pltpu.SemaphoreType.DMA
    vmem = pl.BlockSpec(memory_space=pltpu.VMEM)
    hbm = pl.BlockSpec(memory_space=pl.ANY)
    smem = pl.BlockSpec(memory_space=pltpu.SMEM)
    return pl.pallas_call(
        functools.partial(fused_kernel, n, tn),
        out_shape=jax.ShapeDtypeStruct((rows // tn, n * cols), bf16),
        in_specs=[vmem, hbm, hbm, vmem, vmem, smem, hbm, vmem, hbm],
        out_specs=vmem,
        scratch_shapes=[
            pltpu.VMEM(cached_key_rows.shape, bf16),
            pltpu.VMEM(cached_value_rows.shape, bf16),
            pltpu.VMEM(output_weight.shape, bf16),
            pltpu.VMEM((rows, rows), f32),
            pltpu.VMEM((rows, rows), f32),
            pltpu.VMEM((n, CHUNKS, tn * PIECE, feat), bf16),
            pltpu.VMEM((steps, 2, tn // 2, PIECE, cols), bf16),
            pltpu.VMEM((steps, tn // 2, PIECE, cols), bf16),
            pltpu.VMEM((steps, PIECE, cols), bf16),
            pltpu.VMEM((steps, PIECE, cols), bf16),
            pltpu.VMEM((steps, PIECE, cols), f32),
            pltpu.VMEM((CHUNKS, n, tn, PIECE, 2 * rank), bf16),
            pltpu.VMEM((CHUNKS, n, tn - 1, PIECE, 2 * rank), bf16),
            pltpu.VMEM((CHUNKS, n, n, PIECE, 2 * rank), bf16),
            pltpu.VMEM((n, CHUNKS, PIECE, n * rank), bf16),
            pltpu.VMEM((n, rank, cols), bf16),
            pltpu.VMEM((steps, PIECE, cols), bf16),
            dma((2, CHUNKS, tn)),
            dma,
            dma((2, n, CHUNKS)),
            dma((n, CHUNKS)),
            dma((steps, 2)),
            dma((steps, 2)),
            dma((CHUNKS, n, tn - 1)),
            dma((CHUNKS, n, tn - 1)),
            dma((CHUNKS, n, n - 1)),
            dma((CHUNKS, n, n)),
            dma((n - 1,)),
            dma((n,)),
            dma((n - 1,)),
            dma((n,)),
            dma((n - 1, tn - 1)),
            dma((n - 1, tn - 1)),
            dma,
            dma((steps,)),
            dma((CHUNKS, n)),
        ],
        compiler_params=pltpu.CompilerParams(
            collective_id=0, has_side_effects=True, vmem_limit_bytes=56 * 1024 * 1024
        ),
    )(
        queries,
        cached_key_rows,
        cached_value_rows,
        cached_row_length[None, :],
        row_adapter_index.reshape(1, rows),
        adapter_slot_index,
        output_weight,
        jnp.swapaxes(adapter_down_weight, 1, 2),
        adapter_up_weight,
    )


def per_device(
    queries,
    cached_key_rows,
    cached_value_rows,
    cached_row_length,
    row_adapter_index,
    adapter_slot_index,
    output_weight,
    adapter_down_weight,
    adapter_up_weight,
):
    row_count = queries.shape[0]
    tensor_count = lax.axis_size("tensor")
    owner_count = lax.axis_size("adapter")
    quarter_rows = row_count // tensor_count
    capacity = max(2, 2 * quarter_rows // owner_count)
    context = cached_key_rows.shape[1]
    kv_local = cached_key_rows.shape[2] // HEAD_WIDTH
    query_heads = queries.reshape(row_count, kv_local, -1, HEAD_WIDTH)
    cached_keys = cached_key_rows.reshape(row_count, context, kv_local, HEAD_WIDTH)
    cached_values = cached_value_rows.reshape(row_count, context, kv_local, HEAD_WIDTH)
    logits = jnp.einsum(
        "rgsd,rcgd->rgsc", query_heads, cached_keys, preferred_element_type=jnp.float32
    ) * HEAD_WIDTH ** (-0.5)
    visible = (jnp.arange(context, dtype=jnp.int32)[None, :] < cached_row_length[:, None])[
        :, None, None, :
    ]
    logits = jnp.where(visible, logits, -1e30)
    highest = jnp.max(logits, axis=-1, keepdims=True)
    weights = jnp.exp(logits - highest)
    attention_probs = (weights / jnp.sum(weights, axis=-1, keepdims=True)).astype(jnp.bfloat16)
    attended = jnp.einsum(
        "rgsc,rcgd->rgsd", attention_probs, cached_values, preferred_element_type=jnp.float32
    )
    attended = attended.astype(jnp.bfloat16).reshape(row_count, -1)
    row_adapter = row_adapter_index[:, 0]
    adapter_count = adapter_slot_index.shape[0]
    matches = row_adapter[:, None] == jnp.arange(adapter_count, dtype=jnp.int32)[None, :]
    slot_index = jnp.sum(jnp.where(matches, adapter_slot_index[None, :], 0), axis=1)
    owner_hot = (slot_index[:, None] == jnp.arange(owner_count, dtype=jnp.int32)[None, :]).astype(
        jnp.int32
    )
    owner_hot = owner_hot.reshape(tensor_count, quarter_rows, owner_count)
    position = jnp.cumsum(owner_hot, axis=1) - 1
    placing = owner_hot[..., None] * (
        position[..., None] == jnp.arange(capacity, dtype=jnp.int32)
    ).astype(jnp.int32)
    split_heads = attended.reshape(tensor_count, quarter_rows, -1)
    send_rows = jnp.einsum(
        "qrjc,qrf->jqcf",
        placing.astype(jnp.bfloat16),
        split_heads,
        preferred_element_type=jnp.float32,
    ).astype(jnp.bfloat16)
    received_parts = lax.all_to_all(send_rows, "adapter", split_axis=0, concat_axis=0, tiled=True)
    rank_terms = jnp.einsum(
        "pato,ow->patw", received_parts, adapter_down_weight[0], preferred_element_type=jnp.float32
    )
    own_terms = lax.psum_scatter(rank_terms, "tensor", scatter_dimension=1, tiled=True)[:, 0]
    rank_activation = own_terms.astype(jnp.bfloat16)
    adapter_terms = jnp.einsum(
        "yhl,lq->yhq", rank_activation, adapter_up_weight[0], preferred_element_type=jnp.float32
    )
    panels = jnp.dot(
        lax.all_gather(attended, "adapter", axis=0, tiled=True),
        output_weight,
        preferred_element_type=jnp.float32,
    )
    shares = lax.psum_scatter(
        panels.reshape(owner_count, tensor_count, quarter_rows, -1),
        "tensor",
        scatter_dimension=1,
        tiled=True,
    )
    base_output_block, adapter_block = (
        lax.all_to_all(
            shares.reshape(owner_count, quarter_rows, -1),
            "adapter",
            split_axis=0,
            concat_axis=2,
            tiled=True,
        ),
        lax.all_to_all(adapter_terms, "adapter", split_axis=0, concat_axis=2, tiled=True),
    )
    base_output_rows = base_output_block[0]
    returned_result = adapter_block[0]
    model_width = base_output_rows.shape[1]
    gathered_terms = returned_result.reshape(capacity, owner_count, model_width)
    own_place = lax.dynamic_index_in_dim(
        placing, lax.axis_index("tensor"), 0, keepdims=False
    ).astype(jnp.float32)
    adapter_rows = jnp.einsum(
        "rjc,cjd->rd", own_place, gathered_terms, precision=lax.Precision.HIGHEST
    )
    return (base_output_rows + 2.0 * adapter_rows).astype(jnp.bfloat16)


def solution(mesh):
    short_line = mesh.shape["adapter"] == 4 and mesh.shape["tensor"] == 4
    return jax.shard_map(
        fused if short_line else per_device,
        mesh=mesh,
        in_specs=(
            P(("group", "adapter"), "tensor"),
            P(("group", "adapter"), None, "tensor"),
            P(("group", "adapter"), None, "tensor"),
            P(("group", "adapter")),
            P(("group", "adapter"), None),
            P("group"),
            P("tensor", "adapter"),
            P(("group", "adapter"), "tensor", None),
            P(("group", "adapter"), None, None),
        ),
        out_specs=P(("group", "adapter", "tensor"), None),
        check_vma=False,
    )
```

```python
import functools

import jax
import jax.numpy as jnp
from jax import lax
from jax.experimental import pallas as pl
from jax.experimental.pallas import tpu as pltpu
from jax.sharding import PartitionSpec as P

HEAD_WIDTH = 128
CHUNKS = 2
PIECE = 16


def remote(src, dst, send, recv, axis, index):
    return pltpu.make_async_remote_copy(
        src_ref=src,
        dst_ref=dst,
        send_sem=send,
        recv_sem=recv,
        device_id={axis: index},
        device_id_type=pl.DeviceIdType.MESH,
    )


def mirror(a, s):
    b = a
    bit = 1
    while bit < 4:
        b = b + ((s // bit) % 2) * (bit - 2 * bit * ((a // bit) % 2))
        bit *= 2
    return b


def as_columns(row):
    count = row.shape[1]
    own = lax.broadcasted_iota(jnp.int32, (count, count), 0) == lax.broadcasted_iota(
        jnp.int32, (count, count), 1
    )
    line = jnp.where(own, jnp.broadcast_to(row.astype(jnp.float32), (count, count)), 0.0)
    return jnp.broadcast_to(jnp.sum(line, axis=1, keepdims=True), (count, count))


def attend_rows(q16, k_buf, v_buf, lens16, row0, kv_local, group, context):
    qf = q16.astype(jnp.float32)
    lane = lax.broadcasted_iota(jnp.int32, (8 * group, 2 * context), 1)
    row = lax.broadcasted_iota(jnp.int32, (8 * group, 2 * context), 0) % 8
    own_half = (lane // context) == (row % 2)
    place = lane % context
    pair = row // 2
    out = [[None, None] for _ in range(kv_local * group)]
    for half in range(2):
        q8 = qf[half * 8 : half * 8 + 8]
        lens = jnp.concatenate([lens16[half * 8 : half * 8 + 8]] * group, axis=0)
        visible = own_half & (place.astype(jnp.float32) < lens)
        for g in range(kv_local):
            lanes = slice(g * HEAD_WIDTH, (g + 1) * HEAD_WIDTH)
            qs = jnp.concatenate(
                [
                    q8[:, (g * group + h) * HEAD_WIDTH : (g * group + h + 1) * HEAD_WIDTH]
                    for h in range(group)
                ],
                axis=0,
            ).astype(jnp.bfloat16)
            keys = k_buf[pl.ds(row0 + half * 8, 8), :, lanes].reshape(8 * context, HEAD_WIDTH)
            vals = v_buf[pl.ds(row0 + half * 8, 8), :, lanes].reshape(8 * context, HEAD_WIDTH)
            cross = lax.dot_general(
                qs, keys, (((1,), (1,)), ((), ())), preferred_element_type=jnp.float32
            )
            width = 2 * context
            logits = cross[:, :width]
            for j in range(1, 4):
                logits = jnp.where(pair == j, cross[:, j * width : (j + 1) * width], logits)
            logits = jnp.where(visible, logits * HEAD_WIDTH ** (-0.5), -1e30)
            weights = jnp.exp(logits - jnp.max(logits, axis=1, keepdims=True))
            probs = weights / jnp.sum(weights, axis=1, keepdims=True)
            spread = jnp.concatenate(
                [jnp.where(pair == j, probs, 0.0) for j in range(4)], axis=1
            ).astype(jnp.bfloat16)
            mixed = jnp.dot(spread, vals, preferred_element_type=jnp.float32)
            for h in range(group):
                out[g * group + h][half] = mixed[8 * h : 8 * h + 8]
    return [jnp.concatenate(pair_of, axis=0).astype(jnp.bfloat16) for pair_of in out]


def fused_kernel(
    n,
    tn,
    q_ref,
    k_hbm,
    v_hbm,
    len_ref,
    radp_ref,
    slot_ref,
    w_hbm,
    down_ref,
    up_hbm,
    out_ref,
    k_buf,
    v_buf,
    w_buf,
    lens,
    slots,
    gat,
    part,
    got,
    half,
    other,
    base,
    lows,
    low_got,
    mids,
    masks,
    ups,
    done,
    kv_sem,
    w_sem,
    gs,
    gr,
    rs,
    rr,
    ls,
    lr,
    ms,
    mr,
    ks,
    kr,
    us,
    ur,
    xs,
    xr,
    ol,
    os,
    orr,
):
    a = lax.axis_index("adapter")
    t = lax.axis_index("tensor")
    core, chip = t % 2, t // 2
    core_peer, chip_peer = mirror(t, 1), mirror(t, 2)
    rows, feat = q_ref.shape
    cols = w_hbm.shape[1]
    rank = down_ref.shape[1]
    context = k_hbm.shape[1]
    kv_local = k_hbm.shape[2] // HEAD_WIDTH
    group = feat // (kv_local * HEAD_WIDTH)
    quarter = rows // tn
    share = rank // tn
    steps = CHUNKS * n

    for c in range(CHUNKS):
        for x in range(tn):
            at = pl.ds(x * quarter + c * PIECE, PIECE)
            pltpu.make_async_copy(k_hbm.at[at], k_buf.at[at], kv_sem.at[0, c, x]).start()
            pltpu.make_async_copy(v_hbm.at[at], v_buf.at[at], kv_sem.at[1, c, x]).start()
    w_copy = pltpu.make_async_copy(w_hbm, w_buf, w_sem)
    w_copy.start()
    own_cols = pl.ds(pl.multiple_of(a * cols, 128), cols)
    up_local = pltpu.make_async_copy(up_hbm.at[0, :, own_cols], ups.at[a], ol)
    up_local.start()

    barrier = pltpu.get_barrier_semaphore()
    for d in range(1, n):
        pl.semaphore_signal(
            barrier, inc=1, device_id={"adapter": (a + d) % n}, device_id_type=pl.DeviceIdType.MESH
        )
    for d in range(1, tn):
        pl.semaphore_signal(
            barrier, inc=1, device_id={"tensor": (t + d) % tn}, device_id_type=pl.DeviceIdType.MESH
        )
    pl.semaphore_wait(barrier, n + tn - 2)

    mine = pl.ds(pl.multiple_of(t * share, share), share)
    up_sends = []
    for d in range(1, n):
        to = (a + d) % n
        up_sends.append(
            remote(
                up_hbm.at[0, mine, pl.ds(pl.multiple_of(to * cols, 128), cols)],
                ups.at[a, mine, :],
                us.at[d - 1],
                ur.at[a],
                "adapter",
                to,
            )
        )
        up_sends[-1].start()
    lens[...] = as_columns(len_ref[...])
    named = radp_ref[...]
    slot = jnp.zeros_like(named)
    for k in range(n):
        slot = slot + jnp.where(named == k, slot_ref[k], 0)
    slots[...] = as_columns(slot)
    slot = slots[pl.ds(pl.multiple_of(t * quarter, quarter), quarter), :]
    slot = jnp.concatenate([slot] * (n * rank // rows), axis=1)
    lane_slot = lax.broadcasted_iota(jnp.int32, (quarter, n * rank), 1) // rank
    hot = jnp.where(lane_slot.astype(jnp.float32) == slot, 1.0, 0.0).astype(jnp.bfloat16)
    masks[a] = hot.reshape(CHUNKS, PIECE, n * rank)
    mask_sends = []
    for d in range(1, n):
        to = (a + d) % n
        mask_sends.append(
            remote(masks.at[a], masks.at[a], ks.at[d - 1], kr.at[a], "adapter", to)
        )
        mask_sends[-1].start()

    def up_line(b, c):
        return remote(
            gat.at[b, c], gat.at[b, c], gs.at[0, b, c], gr.at[b, c], "adapter", (a + 1) % n
        )

    def down_line(b, c):
        return remote(
            gat.at[b, c], gat.at[b, c], gs.at[1, b, c], gr.at[b, c], "adapter", (a + n - 1) % n
        )

    for c in range(CHUNKS):

        def attend_step(x, carry, c=c):
            row0 = pl.multiple_of(x * quarter + c * PIECE, PIECE)
            at = pl.ds(row0, PIECE)
            pltpu.make_async_copy(k_hbm.at[at], k_buf.at[at], kv_sem.at[0, c, x]).wait()
            pltpu.make_async_copy(v_hbm.at[at], v_buf.at[at], kv_sem.at[1, c, x]).wait()
            heads = attend_rows(
                q_ref[at, :], k_buf, v_buf, lens[at, :], row0, kv_local, group, context
            )
            to = pl.ds(pl.multiple_of(x * PIECE, PIECE), PIECE)
            for h, value in enumerate(heads):
                gat[a, c, to, h * HEAD_WIDTH : (h + 1) * HEAD_WIDTH] = value
            return carry

        lax.fori_loop(0, tn, attend_step, 0)

        @pl.when((a < n - 1) & (c * a == 0))
        def _(c=c):
            up_line(a, c).start()

        @pl.when((a > 0) & (c * (n - 1 - a) == 0))
        def _(c=c):
            down_line(a, c).start()

    w_copy.wait()

    def part_of(index):
        return pl.ds(pl.multiple_of(index * share, share), share)

    def share_copy(d, k):
        source = (a + d) % n
        at = part_of(chip_peer if k == 2 else t)
        return remote(
            ups.at[source, at, :], ups.at[source, at, :], xs.at[d - 1, k], xr.at[d - 1, k],
            "tensor", chip_peer if k == 1 else core_peer,
        )

    def share_wait(d, k):
        source = (a + d) % n
        at = part_of(mirror(t, k + 1))
        remote(
            ups.at[source, at, :], ups.at[source, at, :], xs.at[d - 1, k], xr.at[d - 1, k],
            "tensor", chip_peer if k == 1 else core_peer,
        ).wait_recv()

    def low_send(c, b, e):
        to = mirror(t, e)
        return remote(
            lows.at[c, b, to], low_got.at[c, b, e - 1], ls.at[c, b, e - 1], lr.at[c, b, e - 1],
            "tensor", to,
        )

    def mid_send(c, b, d):
        return remote(
            mids.at[c, b, a], mids.at[c, b, a], ms.at[c, b, d - 1], mr.at[c, b, a],
            "adapter", (a + d) % n,
        )

    def core_send(i):
        return remote(
            part.at[i, 1 - core], got.at[i], rs.at[i, 0], rr.at[i, 0], "tensor", core_peer
        )

    def chip_send(i):
        return remote(half.at[i], other.at[i], rs.at[i, 1], rr.at[i, 1], "tensor", chip_peer)

    def low(c, b):
        y = lax.dot_general(
            gat[b, c], down_ref[0], (((1,), (1,)), ((), ())), preferred_element_type=jnp.float32
        )
        y = jnp.concatenate([y, jnp.zeros_like(y)], axis=1).astype(jnp.bfloat16)
        lows[c, b] = y.reshape(tn, PIECE, 2 * rank)
        for e in range(1, tn):
            low_send(c, b, e).start()

    def mid(c, b):
        total = lows[c, b, t].astype(jnp.float32)
        for e in range(1, tn):
            low_send(c, b, e).wait_recv()
            total = total + low_got[c, b, e - 1].astype(jnp.float32)
        mids[c, b, a] = total.astype(jnp.bfloat16)
        for d in range(1, n):
            mid_send(c, b, d).start()

    def multiply(i):
        c, j = i // n, i % n
        below = a - j
        above = a + j
        from_below = (below >= 0) & (below < a)
        from_above = (above < n) & (above > a)

        @pl.when(from_above)
        def _():
            down_line(above, c).wait_recv()

            @pl.when(a > 0)
            def _():
                down_line(above, c).start()

        @pl.when(from_below)
        def _():
            up_line(below, c).wait_recv()

            @pl.when(a < n - 1)
            def _():
                up_line(below, c).start()

        @pl.when((i == n - 2) & (a > 0) & (a < n - 1))
        def _():
            up_line(a, 1).start()
            down_line(a, 1).start()

        @pl.when(from_above)
        def _():
            low(c, above)

        @pl.when(from_below)
        def _():
            low(c, below)

        @pl.when(j == 0)
        def _():
            low(c, a)

        x = gat[mirror(a, j), c]
        tile = 512
        for k in range(cols // tile):
            lanes = slice(k * tile, (k + 1) * tile)
            y = jnp.dot(x, w_buf[:, lanes], preferred_element_type=jnp.float32)
            y = y.astype(jnp.bfloat16)
            for piece in range(tn):
                part[i, piece % 2, piece // 2, :, lanes] = y[piece * PIECE : (piece + 1) * PIECE]
        core_send(i).start()

    def ranks(i):
        c, j = i // n, i % n

        @pl.when(j == 0)
        def _():
            mid(c, a)

        @pl.when((j > 0) & (a + j < n))
        def _():
            mid(c, a + j)

        @pl.when((j > 0) & (a - j >= 0))
        def _():
            mid(c, a - j)

    def pair(i):
        core_send(i).wait_recv()
        away = part[i, core, 1 - chip].astype(jnp.float32) + got[i, 1 - chip].astype(jnp.float32)
        half[i] = away.astype(jnp.bfloat16)
        chip_send(i).start()
        base[i] = part[i, core, chip].astype(jnp.float32) + got[i, chip].astype(jnp.float32)

    def add_up(i):
        chip_send(i).wait_recv()
        base[i] = base[i] + other[i].astype(jnp.float32)

    def result(c, j):
        return remote(
            done.at[c * n + j],
            out_ref.at[pl.ds(pl.multiple_of(c * PIECE, PIECE), PIECE), own_cols],
            os.at[c * n + j],
            orr.at[c, a],
            "adapter",
            mirror(a, j),
        )

    def finish(c, j):
        i = c * n + j
        b = mirror(a, j)
        for d in range(1, n):
            source = (a + d) % n
            remote(mids.at[c, b, source], mids.at[c, b, source], ms.at[0, 0, 0],
                   mr.at[c, b, source], "adapter", source).wait_recv()
        low = jnp.concatenate(
            [mids[c, b, k].astype(jnp.float32)[:, :rank] for k in range(n)], axis=1
        )
        low = jnp.where(masks[b, c].astype(jnp.float32) > 0.5, low, 0.0).astype(jnp.bfloat16)
        delta = jnp.dot(
            low, ups[...].reshape(n * rank, cols), preferred_element_type=jnp.float32
        )
        y = (base[i] + 2.0 * delta).astype(jnp.bfloat16)

        @pl.when(j == 0)
        def _():
            out_ref[pl.ds(pl.multiple_of(c * PIECE, PIECE), PIECE), own_cols] = y

        @pl.when(j > 0)
        def _():
            done[i] = y
            result(c, j).start()

    def step(i, carry):
        @pl.when(i < steps)
        def _():
            multiply(i)

        @pl.when(i == 1)
        def _():
            for d in range(1, n):
                source = (a + d) % n
                remote(ups.at[source, mine, :], ups.at[source, mine, :], us.at[0], ur.at[source],
                       "adapter", source).wait_recv()
                share_copy(d, 0).start()
                share_copy(d, 1).start()

        @pl.when(i == 3)
        def _():
            for d in range(1, n):
                share_wait(d, 1)
                share_copy(d, 2).start()

        @pl.when((i > 0) & (i <= steps))
        def _():
            ranks(i - 1)
            pair(i - 1)

        @pl.when(i > 1)
        def _():
            add_up(i - 2)

        @pl.when(i == n)
        def _():
            up_local.wait()
            for d in range(1, n):
                source = (a + d) % n
                remote(masks.at[source], masks.at[source], ks.at[0], kr.at[source],
                       "adapter", source).wait_recv()
                share_wait(d, 0)
                share_wait(d, 2)

        @pl.when((i == n + 2) | (i == n + 3))
        def _():
            def early(k, inner):
                finish(0, (i - n - 2) * 2 + k)
                return inner

            lax.fori_loop(0, 2, early, 0)

        return carry

    lax.fori_loop(0, steps + 1, step, 0)

    def last(k, carry):
        late = k // 2

        @pl.when(k == 2)
        def _():
            add_up(steps - 1)

        finish(1, (1 - late) * (2 - k) + late * (9 - 3 * k))
        return carry

    lax.fori_loop(0, n, last, 0)

    for c in range(CHUNKS):
        for d in range(1, n):
            source = (a + d) % n
            there = pl.ds(pl.multiple_of(source * cols, 128), cols)
            remote(done.at[0], out_ref.at[pl.ds(c * PIECE, PIECE), there], os.at[0],
                   orr.at[c, source], "adapter", source).wait_recv()
    for copy in up_sends + mask_sends:
        copy.wait_send()
    for d in range(1, n):
        for k in range(3):
            share_copy(d, k).wait_send()

    def settle(i, carry):
        c, s = i // n, i % n
        core_send(i).wait_send()
        chip_send(i).wait_send()
        for e in range(1, tn):
            low_send(c, s, e).wait_send()
        for d in range(1, n):
            mid_send(c, s, d).wait_send()

        @pl.when(s > 0)
        def _():
            result(c, s).wait_send()

        @pl.when((s <= a) & (a < n - 1))
        def _():
            up_line(s, c).wait_send()

        @pl.when((s >= a) & (a > 0))
        def _():
            down_line(s, c).wait_send()

        return carry

    lax.fori_loop(0, steps, settle, 0)


def fused(
    queries,
    cached_key_rows,
    cached_value_rows,
    cached_row_length,
    row_adapter_index,
    adapter_slot_index,
    output_weight,
    adapter_down_weight,
    adapter_up_weight,
):
    n, tn = lax.axis_size("adapter"), lax.axis_size("tensor")
    rows, feat = queries.shape
    cols = output_weight.shape[1]
    rank = adapter_down_weight.shape[2]
    steps = CHUNKS * n
    bf16, f32 = jnp.bfloat16, jnp.float32
    dma = pltpu.SemaphoreType.DMA
    vmem = pl.BlockSpec(memory_space=pltpu.VMEM)
    hbm = pl.BlockSpec(memory_space=pl.ANY)
    smem = pl.BlockSpec(memory_space=pltpu.SMEM)
    return pl.pallas_call(
        functools.partial(fused_kernel, n, tn),
        out_shape=jax.ShapeDtypeStruct((rows // tn, n * cols), bf16),
        in_specs=[vmem, hbm, hbm, vmem, vmem, smem, hbm, vmem, hbm],
        out_specs=vmem,
        scratch_shapes=[
            pltpu.VMEM(cached_key_rows.shape, bf16),
            pltpu.VMEM(cached_value_rows.shape, bf16),
            pltpu.VMEM(output_weight.shape, bf16),
            pltpu.VMEM((rows, rows), f32),
            pltpu.VMEM((rows, rows), f32),
            pltpu.VMEM((n, CHUNKS, tn * PIECE, feat), bf16),
            pltpu.VMEM((steps, 2, tn // 2, PIECE, cols), bf16),
            pltpu.VMEM((steps, tn // 2, PIECE, cols), bf16),
            pltpu.VMEM((steps, PIECE, cols), bf16),
            pltpu.VMEM((steps, PIECE, cols), bf16),
            pltpu.VMEM((steps, PIECE, cols), f32),
            pltpu.VMEM((CHUNKS, n, tn, PIECE, 2 * rank), bf16),
            pltpu.VMEM((CHUNKS, n, tn - 1, PIECE, 2 * rank), bf16),
            pltpu.VMEM((CHUNKS, n, n, PIECE, 2 * rank), bf16),
            pltpu.VMEM((n, CHUNKS, PIECE, n * rank), bf16),
            pltpu.VMEM((n, rank, cols), bf16),
            pltpu.VMEM((steps, PIECE, cols), bf16),
            dma((2, CHUNKS, tn)),
            dma,
            dma((2, n, CHUNKS)),
            dma((n, CHUNKS)),
            dma((steps, 2)),
            dma((steps, 2)),
            dma((CHUNKS, n, tn - 1)),
            dma((CHUNKS, n, tn - 1)),
            dma((CHUNKS, n, n - 1)),
            dma((CHUNKS, n, n)),
            dma((n - 1,)),
            dma((n,)),
            dma((n - 1,)),
            dma((n,)),
            dma((n - 1, tn - 1)),
            dma((n - 1, tn - 1)),
            dma,
            dma((steps,)),
            dma((CHUNKS, n)),
        ],
        compiler_params=pltpu.CompilerParams(
            collective_id=0, has_side_effects=True, vmem_limit_bytes=56 * 1024 * 1024
        ),
    )(
        queries,
        cached_key_rows,
        cached_value_rows,
        cached_row_length[None, :],
        row_adapter_index.reshape(1, rows),
        adapter_slot_index,
        output_weight,
        jnp.swapaxes(adapter_down_weight, 1, 2),
        adapter_up_weight,
    )


def per_device(
    queries,
    cached_key_rows,
    cached_value_rows,
    cached_row_length,
    row_adapter_index,
    adapter_slot_index,
    output_weight,
    adapter_down_weight,
    adapter_up_weight,
):
    row_count = queries.shape[0]
    tensor_count = lax.axis_size("tensor")
    owner_count = lax.axis_size("adapter")
    quarter_rows = row_count // tensor_count
    capacity = max(2, 2 * quarter_rows // owner_count)
    context = cached_key_rows.shape[1]
    kv_local = cached_key_rows.shape[2] // HEAD_WIDTH
    query_heads = queries.reshape(row_count, kv_local, -1, HEAD_WIDTH)
    cached_keys = cached_key_rows.reshape(row_count, context, kv_local, HEAD_WIDTH)
    cached_values = cached_value_rows.reshape(row_count, context, kv_local, HEAD_WIDTH)
    logits = jnp.einsum(
        "rgsd,rcgd->rgsc", query_heads, cached_keys, preferred_element_type=jnp.float32
    ) * HEAD_WIDTH ** (-0.5)
    visible = (jnp.arange(context, dtype=jnp.int32)[None, :] < cached_row_length[:, None])[
        :, None, None, :
    ]
    logits = jnp.where(visible, logits, -1e30)
    highest = jnp.max(logits, axis=-1, keepdims=True)
    weights = jnp.exp(logits - highest)
    attention_probs = (weights / jnp.sum(weights, axis=-1, keepdims=True)).astype(jnp.bfloat16)
    attended = jnp.einsum(
        "rgsc,rcgd->rgsd", attention_probs, cached_values, preferred_element_type=jnp.float32
    )
    attended = attended.astype(jnp.bfloat16).reshape(row_count, -1)
    row_adapter = row_adapter_index[:, 0]
    adapter_count = adapter_slot_index.shape[0]
    matches = row_adapter[:, None] == jnp.arange(adapter_count, dtype=jnp.int32)[None, :]
    slot_index = jnp.sum(jnp.where(matches, adapter_slot_index[None, :], 0), axis=1)
    owner_hot = (slot_index[:, None] == jnp.arange(owner_count, dtype=jnp.int32)[None, :]).astype(
        jnp.int32
    )
    owner_hot = owner_hot.reshape(tensor_count, quarter_rows, owner_count)
    position = jnp.cumsum(owner_hot, axis=1) - 1
    placing = owner_hot[..., None] * (
        position[..., None] == jnp.arange(capacity, dtype=jnp.int32)
    ).astype(jnp.int32)
    split_heads = attended.reshape(tensor_count, quarter_rows, -1)
    send_rows = jnp.einsum(
        "qrjc,qrf->jqcf",
        placing.astype(jnp.bfloat16),
        split_heads,
        preferred_element_type=jnp.float32,
    ).astype(jnp.bfloat16)
    received_parts = lax.all_to_all(send_rows, "adapter", split_axis=0, concat_axis=0, tiled=True)
    rank_terms = jnp.einsum(
        "pato,ow->patw", received_parts, adapter_down_weight[0], preferred_element_type=jnp.float32
    )
    own_terms = lax.psum_scatter(rank_terms, "tensor", scatter_dimension=1, tiled=True)[:, 0]
    rank_activation = own_terms.astype(jnp.bfloat16)
    adapter_terms = jnp.einsum(
        "yhl,lq->yhq", rank_activation, adapter_up_weight[0], preferred_element_type=jnp.float32
    )
    panels = jnp.dot(
        lax.all_gather(attended, "adapter", axis=0, tiled=True),
        output_weight,
        preferred_element_type=jnp.float32,
    )
    shares = lax.psum_scatter(
        panels.reshape(owner_count, tensor_count, quarter_rows, -1),
        "tensor",
        scatter_dimension=1,
        tiled=True,
    )
    base_output_block, adapter_block = (
        lax.all_to_all(
            shares.reshape(owner_count, quarter_rows, -1),
            "adapter",
            split_axis=0,
            concat_axis=2,
            tiled=True,
        ),
        lax.all_to_all(adapter_terms, "adapter", split_axis=0, concat_axis=2, tiled=True),
    )
    base_output_rows = base_output_block[0]
    returned_result = adapter_block[0]
    model_width = base_output_rows.shape[1]
    gathered_terms = returned_result.reshape(capacity, owner_count, model_width)
    own_place = lax.dynamic_index_in_dim(
        placing, lax.axis_index("tensor"), 0, keepdims=False
    ).astype(jnp.float32)
    adapter_rows = jnp.einsum(
        "rjc,cjd->rd", own_place, gathered_terms, precision=lax.Precision.HIGHEST
    )
    return (base_output_rows + 2.0 * adapter_rows).astype(jnp.bfloat16)


def solution(mesh):
    short_line = mesh.shape["adapter"] == 4 and mesh.shape["tensor"] == 4
    return jax.shard_map(
        fused if short_line else per_device,
        mesh=mesh,
        in_specs=(
            P(("group", "adapter"), "tensor"),
            P(("group", "adapter"), None, "tensor"),
            P(("group", "adapter"), None, "tensor"),
            P(("group", "adapter")),
            P(("group", "adapter"), None),
            P("group"),
            P("tensor", "adapter"),
            P(("group", "adapter"), "tensor", None),
            P(("group", "adapter"), None, None),
        ),
        out_specs=P(("group", "adapter", "tensor"), None),
        check_vma=False,
    )
```

```python
import functools

import jax
import jax.numpy as jnp
from jax import lax
from jax.experimental import pallas as pl
from jax.experimental.pallas import tpu as pltpu
from jax.sharding import PartitionSpec as P

HEAD_WIDTH = 128
CHUNKS = 2
PIECE = 16


def remote(src, dst, send, recv, axis, index):
    return pltpu.make_async_remote_copy(
        src_ref=src,
        dst_ref=dst,
        send_sem=send,
        recv_sem=recv,
        device_id={axis: index},
        device_id_type=pl.DeviceIdType.MESH,
    )


def mirror(a, s):
    b = a
    bit = 1
    while bit < 4:
        b = b + ((s // bit) % 2) * (bit - 2 * bit * ((a // bit) % 2))
        bit *= 2
    return b


def as_columns(row):
    count = row.shape[1]
    own = lax.broadcasted_iota(jnp.int32, (count, count), 0) == lax.broadcasted_iota(
        jnp.int32, (count, count), 1
    )
    line = jnp.where(own, jnp.broadcast_to(row.astype(jnp.float32), (count, count)), 0.0)
    return jnp.broadcast_to(jnp.sum(line, axis=1, keepdims=True), (count, count))


def attend_rows(q16, k_buf, v_buf, lens16, row0, kv_local, group, context):
    qf = q16.astype(jnp.float32)
    lane = lax.broadcasted_iota(jnp.int32, (8 * group, 2 * context), 1)
    row = lax.broadcasted_iota(jnp.int32, (8 * group, 2 * context), 0) % 8
    own_half = (lane // context) == (row % 2)
    place = lane % context
    pair = row // 2
    out = [[None, None] for _ in range(kv_local * group)]
    for half in range(2):
        q8 = qf[half * 8 : half * 8 + 8]
        lens = jnp.concatenate([lens16[half * 8 : half * 8 + 8]] * group, axis=0)
        visible = own_half & (place.astype(jnp.float32) < lens)
        for g in range(kv_local):
            lanes = slice(g * HEAD_WIDTH, (g + 1) * HEAD_WIDTH)
            qs = jnp.concatenate(
                [
                    q8[:, (g * group + h) * HEAD_WIDTH : (g * group + h + 1) * HEAD_WIDTH]
                    for h in range(group)
                ],
                axis=0,
            ).astype(jnp.bfloat16)
            keys = k_buf[pl.ds(row0 + half * 8, 8), :, lanes].reshape(8 * context, HEAD_WIDTH)
            vals = v_buf[pl.ds(row0 + half * 8, 8), :, lanes].reshape(8 * context, HEAD_WIDTH)
            cross = lax.dot_general(
                qs, keys, (((1,), (1,)), ((), ())), preferred_element_type=jnp.float32
            )
            width = 2 * context
            logits = cross[:, :width]
            for j in range(1, 4):
                logits = jnp.where(pair == j, cross[:, j * width : (j + 1) * width], logits)
            logits = jnp.where(visible, logits * HEAD_WIDTH ** (-0.5), -1e30)
            weights = jnp.exp(logits - jnp.max(logits, axis=1, keepdims=True))
            probs = weights / jnp.sum(weights, axis=1, keepdims=True)
            spread = jnp.concatenate(
                [jnp.where(pair == j, probs, 0.0) for j in range(4)], axis=1
            ).astype(jnp.bfloat16)
            mixed = jnp.dot(spread, vals, preferred_element_type=jnp.float32)
            for h in range(group):
                out[g * group + h][half] = mixed[8 * h : 8 * h + 8]
    return [jnp.concatenate(pair_of, axis=0).astype(jnp.bfloat16) for pair_of in out]


def fused_kernel(
    n,
    tn,
    q_ref,
    k_hbm,
    v_hbm,
    len_ref,
    radp_ref,
    slot_ref,
    w_hbm,
    down_ref,
    up_hbm,
    out_ref,
    k_buf,
    v_buf,
    w_buf,
    lens,
    slots,
    gat,
    part,
    got,
    half,
    other,
    base,
    lows,
    low_got,
    mids,
    masks,
    ups,
    done,
    kv_sem,
    w_sem,
    gs,
    gr,
    rs,
    rr,
    ls,
    lr,
    ms,
    mr,
    ks,
    kr,
    us,
    ur,
    xs,
    xr,
    ol,
    os,
    orr,
):
    a = lax.axis_index("adapter")
    t = lax.axis_index("tensor")
    core, chip = t % 2, t // 2
    core_peer, chip_peer = mirror(t, 1), mirror(t, 2)
    rows, feat = q_ref.shape
    cols = w_hbm.shape[1]
    rank = down_ref.shape[1]
    context = k_hbm.shape[1]
    kv_local = k_hbm.shape[2] // HEAD_WIDTH
    group = feat // (kv_local * HEAD_WIDTH)
    quarter = rows // tn
    share = rank // tn
    steps = CHUNKS * n

    for c in range(CHUNKS):
        for x in range(tn):
            at = pl.ds(x * quarter + c * PIECE, PIECE)
            pltpu.make_async_copy(k_hbm.at[at], k_buf.at[at], kv_sem.at[0, c, x]).start()
            pltpu.make_async_copy(v_hbm.at[at], v_buf.at[at], kv_sem.at[1, c, x]).start()
    w_copy = pltpu.make_async_copy(w_hbm, w_buf, w_sem)
    w_copy.start()
    own_cols = pl.ds(pl.multiple_of(a * cols, 128), cols)
    up_local = pltpu.make_async_copy(up_hbm.at[0, :, own_cols], ups.at[a], ol)
    up_local.start()

    barrier = pltpu.get_barrier_semaphore()
    for d in range(1, n):
        pl.semaphore_signal(
            barrier, inc=1, device_id={"adapter": (a + d) % n}, device_id_type=pl.DeviceIdType.MESH
        )
    for d in range(1, tn):
        pl.semaphore_signal(
            barrier, inc=1, device_id={"tensor": (t + d) % tn}, device_id_type=pl.DeviceIdType.MESH
        )
    pl.semaphore_wait(barrier, n + tn - 2)

    mine = pl.ds(pl.multiple_of(t * share, share), share)
    up_sends = []
    for d in range(1, n):
        to = (a + d) % n
        up_sends.append(
            remote(
                up_hbm.at[0, mine, pl.ds(pl.multiple_of(to * cols, 128), cols)],
                ups.at[a, mine, :],
                us.at[d - 1],
                ur.at[a],
                "adapter",
                to,
            )
        )
        up_sends[-1].start()
    lens[...] = as_columns(len_ref[...])
    named = radp_ref[...]
    slot = jnp.zeros_like(named)
    for k in range(n):
        slot = slot + jnp.where(named == k, slot_ref[k], 0)
    slots[...] = as_columns(slot)
    slot = slots[pl.ds(pl.multiple_of(t * quarter, quarter), quarter), :]
    slot = jnp.concatenate([slot] * (n * rank // rows), axis=1)
    lane_slot = lax.broadcasted_iota(jnp.int32, (quarter, n * rank), 1) // rank
    hot = jnp.where(lane_slot.astype(jnp.float32) == slot, 1.0, 0.0).astype(jnp.bfloat16)
    masks[a] = hot.reshape(CHUNKS, PIECE, n * rank)
    mask_sends = []
    for d in range(1, n):
        to = (a + d) % n
        mask_sends.append(
            remote(masks.at[a], masks.at[a], ks.at[d - 1], kr.at[a], "adapter", to)
        )
        mask_sends[-1].start()

    def up_line(b, c):
        return remote(
            gat.at[b, c], gat.at[b, c], gs.at[0, b, c], gr.at[b, c], "adapter", (a + 1) % n
        )

    def down_line(b, c):
        return remote(
            gat.at[b, c], gat.at[b, c], gs.at[1, b, c], gr.at[b, c], "adapter", (a + n - 1) % n
        )

    for c in range(CHUNKS):

        def attend_step(x, carry, c=c):
            row0 = pl.multiple_of(x * quarter + c * PIECE, PIECE)
            at = pl.ds(row0, PIECE)
            pltpu.make_async_copy(k_hbm.at[at], k_buf.at[at], kv_sem.at[0, c, x]).wait()
            pltpu.make_async_copy(v_hbm.at[at], v_buf.at[at], kv_sem.at[1, c, x]).wait()
            heads = attend_rows(
                q_ref[at, :], k_buf, v_buf, lens[at, :], row0, kv_local, group, context
            )
            to = pl.ds(pl.multiple_of(x * PIECE, PIECE), PIECE)
            for h, value in enumerate(heads):
                gat[a, c, to, h * HEAD_WIDTH : (h + 1) * HEAD_WIDTH] = value
            return carry

        lax.fori_loop(0, tn, attend_step, 0)

        @pl.when((a < n - 1) & (c * a == 0))
        def _(c=c):
            up_line(a, c).start()

        @pl.when((a > 0) & (c * (n - 1 - a) == 0))
        def _(c=c):
            down_line(a, c).start()

    w_copy.wait()

    def part_of(index):
        return pl.ds(pl.multiple_of(index * share, share), share)

    def share_copy(d, k):
        source = (a + d) % n
        at = part_of(chip_peer if k == 2 else t)
        return remote(
            ups.at[source, at, :], ups.at[source, at, :], xs.at[d - 1, k], xr.at[d - 1, k],
            "tensor", chip_peer if k == 1 else core_peer,
        )

    def share_wait(d, k):
        source = (a + d) % n
        at = part_of(mirror(t, k + 1))
        remote(
            ups.at[source, at, :], ups.at[source, at, :], xs.at[d - 1, k], xr.at[d - 1, k],
            "tensor", chip_peer if k == 1 else core_peer,
        ).wait_recv()

    def low_send(c, b, e):
        to = mirror(t, e)
        return remote(
            lows.at[c, b, to], low_got.at[c, b, e - 1], ls.at[c, b, e - 1], lr.at[c, b, e - 1],
            "tensor", to,
        )

    def mid_send(c, b, d):
        return remote(
            mids.at[c, b, a], mids.at[c, b, a], ms.at[c, b, d - 1], mr.at[c, b, a],
            "adapter", (a + d) % n,
        )

    def core_send(i):
        return remote(
            part.at[i, 1 - core], got.at[i], rs.at[i, 0], rr.at[i, 0], "tensor", core_peer
        )

    def chip_send(i):
        return remote(half.at[i], other.at[i], rs.at[i, 1], rr.at[i, 1], "tensor", chip_peer)

    def low(c, b):
        y = lax.dot_general(
            gat[b, c], down_ref[0], (((1,), (1,)), ((), ())), preferred_element_type=jnp.float32
        )
        y = jnp.concatenate([y, jnp.zeros_like(y)], axis=1).astype(jnp.bfloat16)
        lows[c, b] = y.reshape(tn, PIECE, 2 * rank)
        for e in range(1, tn):
            low_send(c, b, e).start()

    def mid(c, b):
        total = lows[c, b, t].astype(jnp.float32)
        for e in range(1, tn):
            low_send(c, b, e).wait_recv()
            total = total + low_got[c, b, e - 1].astype(jnp.float32)
        mids[c, b, a] = total.astype(jnp.bfloat16)
        for d in range(1, n):
            mid_send(c, b, d).start()

    def multiply(i):
        c, j = i // n, i % n
        below = a - j
        above = a + j
        from_below = (below >= 0) & (below < a)
        from_above = (above < n) & (above > a)

        @pl.when(from_above)
        def _():
            down_line(above, c).wait_recv()

            @pl.when(a > 0)
            def _():
                down_line(above, c).start()

        @pl.when(from_below)
        def _():
            up_line(below, c).wait_recv()

            @pl.when(a < n - 1)
            def _():
                up_line(below, c).start()

        @pl.when((i == n - 3) & (a > 0) & (a < n - 1))
        def _():
            up_line(a, 1).start()
            down_line(a, 1).start()

        @pl.when(from_above)
        def _():
            low(c, above)

        @pl.when(from_below)
        def _():
            low(c, below)

        @pl.when(j == 0)
        def _():
            low(c, a)

        x = gat[mirror(a, j), c]
        tile = 512
        for k in range(cols // tile):
            lanes = slice(k * tile, (k + 1) * tile)
            y = jnp.dot(x, w_buf[:, lanes], preferred_element_type=jnp.float32)
            y = y.astype(jnp.bfloat16)
            for piece in range(tn):
                part[i, piece % 2, piece // 2, :, lanes] = y[piece * PIECE : (piece + 1) * PIECE]
        core_send(i).start()

    def ranks(i):
        c, j = i // n, i % n

        @pl.when(j == 0)
        def _():
            mid(c, a)

        @pl.when((j > 0) & (a + j < n))
        def _():
            mid(c, a + j)

        @pl.when((j > 0) & (a - j >= 0))
        def _():
            mid(c, a - j)

    def pair(i):
        core_send(i).wait_recv()
        away = part[i, core, 1 - chip].astype(jnp.float32) + got[i, 1 - chip].astype(jnp.float32)
        half[i] = away.astype(jnp.bfloat16)
        chip_send(i).start()
        base[i] = part[i, core, chip].astype(jnp.float32) + got[i, chip].astype(jnp.float32)

    def add_up(i):
        chip_send(i).wait_recv()
        base[i] = base[i] + other[i].astype(jnp.float32)

    def result(c, j):
        return remote(
            done.at[c * n + j],
            out_ref.at[pl.ds(pl.multiple_of(c * PIECE, PIECE), PIECE), own_cols],
            os.at[c * n + j],
            orr.at[c, a],
            "adapter",
            mirror(a, j),
        )

    def finish(c, j):
        i = c * n + j
        b = mirror(a, j)
        for d in range(1, n):
            source = (a + d) % n
            remote(mids.at[c, b, source], mids.at[c, b, source], ms.at[0, 0, 0],
                   mr.at[c, b, source], "adapter", source).wait_recv()
        low = jnp.concatenate(
            [mids[c, b, k].astype(jnp.float32)[:, :rank] for k in range(n)], axis=1
        )
        low = jnp.where(masks[b, c].astype(jnp.float32) > 0.5, low, 0.0).astype(jnp.bfloat16)
        delta = jnp.dot(
            low, ups[...].reshape(n * rank, cols), preferred_element_type=jnp.float32
        )
        y = (base[i] + 2.0 * delta).astype(jnp.bfloat16)

        @pl.when(j == 0)
        def _():
            out_ref[pl.ds(pl.multiple_of(c * PIECE, PIECE), PIECE), own_cols] = y

        @pl.when(j > 0)
        def _():
            done[i] = y
            result(c, j).start()

    def step(i, carry):
        @pl.when(i < steps)
        def _():
            multiply(i)

        @pl.when(i == 1)
        def _():
            for d in range(1, n):
                source = (a + d) % n
                remote(ups.at[source, mine, :], ups.at[source, mine, :], us.at[0], ur.at[source],
                       "adapter", source).wait_recv()
                share_copy(d, 0).start()
                share_copy(d, 1).start()

        @pl.when(i == 3)
        def _():
            for d in range(1, n):
                share_wait(d, 1)
                share_copy(d, 2).start()

        @pl.when((i > 0) & (i <= steps))
        def _():
            ranks(i - 1)
            pair(i - 1)

        @pl.when(i > 1)
        def _():
            add_up(i - 2)

        @pl.when(i == n)
        def _():
            up_local.wait()
            for d in range(1, n):
                source = (a + d) % n
                remote(masks.at[source], masks.at[source], ks.at[0], kr.at[source],
                       "adapter", source).wait_recv()
                share_wait(d, 0)
                share_wait(d, 2)

        @pl.when((i == n + 2) | (i == n + 3))
        def _():
            def early(k, inner):
                finish(0, (i - n - 2) * 2 + k)
                return inner

            lax.fori_loop(0, 2, early, 0)

        return carry

    lax.fori_loop(0, steps + 1, step, 0)

    def last(k, carry):
        late = k // 2

        @pl.when(k == 2)
        def _():
            add_up(steps - 1)

        finish(1, (1 - late) * (2 - k) + late * (9 - 3 * k))
        return carry

    lax.fori_loop(0, n, last, 0)

    for c in range(CHUNKS):
        for d in range(1, n):
            source = (a + d) % n
            there = pl.ds(pl.multiple_of(source * cols, 128), cols)
            remote(done.at[0], out_ref.at[pl.ds(c * PIECE, PIECE), there], os.at[0],
                   orr.at[c, source], "adapter", source).wait_recv()
    for copy in up_sends + mask_sends:
        copy.wait_send()
    for d in range(1, n):
        for k in range(3):
            share_copy(d, k).wait_send()

    def settle(i, carry):
        c, s = i // n, i % n
        core_send(i).wait_send()
        chip_send(i).wait_send()
        for e in range(1, tn):
            low_send(c, s, e).wait_send()
        for d in range(1, n):
            mid_send(c, s, d).wait_send()

        @pl.when(s > 0)
        def _():
            result(c, s).wait_send()

        @pl.when((s <= a) & (a < n - 1))
        def _():
            up_line(s, c).wait_send()

        @pl.when((s >= a) & (a > 0))
        def _():
            down_line(s, c).wait_send()

        return carry

    lax.fori_loop(0, steps, settle, 0)


def fused(
    queries,
    cached_key_rows,
    cached_value_rows,
    cached_row_length,
    row_adapter_index,
    adapter_slot_index,
    output_weight,
    adapter_down_weight,
    adapter_up_weight,
):
    n, tn = lax.axis_size("adapter"), lax.axis_size("tensor")
    rows, feat = queries.shape
    cols = output_weight.shape[1]
    rank = adapter_down_weight.shape[2]
    steps = CHUNKS * n
    bf16, f32 = jnp.bfloat16, jnp.float32
    dma = pltpu.SemaphoreType.DMA
    vmem = pl.BlockSpec(memory_space=pltpu.VMEM)
    hbm = pl.BlockSpec(memory_space=pl.ANY)
    smem = pl.BlockSpec(memory_space=pltpu.SMEM)
    return pl.pallas_call(
        functools.partial(fused_kernel, n, tn),
        out_shape=jax.ShapeDtypeStruct((rows // tn, n * cols), bf16),
        in_specs=[vmem, hbm, hbm, vmem, vmem, smem, hbm, vmem, hbm],
        out_specs=vmem,
        scratch_shapes=[
            pltpu.VMEM(cached_key_rows.shape, bf16),
            pltpu.VMEM(cached_value_rows.shape, bf16),
            pltpu.VMEM(output_weight.shape, bf16),
            pltpu.VMEM((rows, rows), f32),
            pltpu.VMEM((rows, rows), f32),
            pltpu.VMEM((n, CHUNKS, tn * PIECE, feat), bf16),
            pltpu.VMEM((steps, 2, tn // 2, PIECE, cols), bf16),
            pltpu.VMEM((steps, tn // 2, PIECE, cols), bf16),
            pltpu.VMEM((steps, PIECE, cols), bf16),
            pltpu.VMEM((steps, PIECE, cols), bf16),
            pltpu.VMEM((steps, PIECE, cols), f32),
            pltpu.VMEM((CHUNKS, n, tn, PIECE, 2 * rank), bf16),
            pltpu.VMEM((CHUNKS, n, tn - 1, PIECE, 2 * rank), bf16),
            pltpu.VMEM((CHUNKS, n, n, PIECE, 2 * rank), bf16),
            pltpu.VMEM((n, CHUNKS, PIECE, n * rank), bf16),
            pltpu.VMEM((n, rank, cols), bf16),
            pltpu.VMEM((steps, PIECE, cols), bf16),
            dma((2, CHUNKS, tn)),
            dma,
            dma((2, n, CHUNKS)),
            dma((n, CHUNKS)),
            dma((steps, 2)),
            dma((steps, 2)),
            dma((CHUNKS, n, tn - 1)),
            dma((CHUNKS, n, tn - 1)),
            dma((CHUNKS, n, n - 1)),
            dma((CHUNKS, n, n)),
            dma((n - 1,)),
            dma((n,)),
            dma((n - 1,)),
            dma((n,)),
            dma((n - 1, tn - 1)),
            dma((n - 1, tn - 1)),
            dma,
            dma((steps,)),
            dma((CHUNKS, n)),
        ],
        compiler_params=pltpu.CompilerParams(
            collective_id=0, has_side_effects=True, vmem_limit_bytes=56 * 1024 * 1024
        ),
    )(
        queries,
        cached_key_rows,
        cached_value_rows,
        cached_row_length[None, :],
        row_adapter_index.reshape(1, rows),
        adapter_slot_index,
        output_weight,
        jnp.swapaxes(adapter_down_weight, 1, 2),
        adapter_up_weight,
    )


def per_device(
    queries,
    cached_key_rows,
    cached_value_rows,
    cached_row_length,
    row_adapter_index,
    adapter_slot_index,
    output_weight,
    adapter_down_weight,
    adapter_up_weight,
):
    row_count = queries.shape[0]
    tensor_count = lax.axis_size("tensor")
    owner_count = lax.axis_size("adapter")
    quarter_rows = row_count // tensor_count
    capacity = max(2, 2 * quarter_rows // owner_count)
    context = cached_key_rows.shape[1]
    kv_local = cached_key_rows.shape[2] // HEAD_WIDTH
    query_heads = queries.reshape(row_count, kv_local, -1, HEAD_WIDTH)
    cached_keys = cached_key_rows.reshape(row_count, context, kv_local, HEAD_WIDTH)
    cached_values = cached_value_rows.reshape(row_count, context, kv_local, HEAD_WIDTH)
    logits = jnp.einsum(
        "rgsd,rcgd->rgsc", query_heads, cached_keys, preferred_element_type=jnp.float32
    ) * HEAD_WIDTH ** (-0.5)
    visible = (jnp.arange(context, dtype=jnp.int32)[None, :] < cached_row_length[:, None])[
        :, None, None, :
    ]
    logits = jnp.where(visible, logits, -1e30)
    highest = jnp.max(logits, axis=-1, keepdims=True)
    weights = jnp.exp(logits - highest)
    attention_probs = (weights / jnp.sum(weights, axis=-1, keepdims=True)).astype(jnp.bfloat16)
    attended = jnp.einsum(
        "rgsc,rcgd->rgsd", attention_probs, cached_values, preferred_element_type=jnp.float32
    )
    attended = attended.astype(jnp.bfloat16).reshape(row_count, -1)
    row_adapter = row_adapter_index[:, 0]
    adapter_count = adapter_slot_index.shape[0]
    matches = row_adapter[:, None] == jnp.arange(adapter_count, dtype=jnp.int32)[None, :]
    slot_index = jnp.sum(jnp.where(matches, adapter_slot_index[None, :], 0), axis=1)
    owner_hot = (slot_index[:, None] == jnp.arange(owner_count, dtype=jnp.int32)[None, :]).astype(
        jnp.int32
    )
    owner_hot = owner_hot.reshape(tensor_count, quarter_rows, owner_count)
    position = jnp.cumsum(owner_hot, axis=1) - 1
    placing = owner_hot[..., None] * (
        position[..., None] == jnp.arange(capacity, dtype=jnp.int32)
    ).astype(jnp.int32)
    split_heads = attended.reshape(tensor_count, quarter_rows, -1)
    send_rows = jnp.einsum(
        "qrjc,qrf->jqcf",
        placing.astype(jnp.bfloat16),
        split_heads,
        preferred_element_type=jnp.float32,
    ).astype(jnp.bfloat16)
    received_parts = lax.all_to_all(send_rows, "adapter", split_axis=0, concat_axis=0, tiled=True)
    rank_terms = jnp.einsum(
        "pato,ow->patw", received_parts, adapter_down_weight[0], preferred_element_type=jnp.float32
    )
    own_terms = lax.psum_scatter(rank_terms, "tensor", scatter_dimension=1, tiled=True)[:, 0]
    rank_activation = own_terms.astype(jnp.bfloat16)
    adapter_terms = jnp.einsum(
        "yhl,lq->yhq", rank_activation, adapter_up_weight[0], preferred_element_type=jnp.float32
    )
    panels = jnp.dot(
        lax.all_gather(attended, "adapter", axis=0, tiled=True),
        output_weight,
        preferred_element_type=jnp.float32,
    )
    shares = lax.psum_scatter(
        panels.reshape(owner_count, tensor_count, quarter_rows, -1),
        "tensor",
        scatter_dimension=1,
        tiled=True,
    )
    base_output_block, adapter_block = (
        lax.all_to_all(
            shares.reshape(owner_count, quarter_rows, -1),
            "adapter",
            split_axis=0,
            concat_axis=2,
            tiled=True,
        ),
        lax.all_to_all(adapter_terms, "adapter", split_axis=0, concat_axis=2, tiled=True),
    )
    base_output_rows = base_output_block[0]
    returned_result = adapter_block[0]
    model_width = base_output_rows.shape[1]
    gathered_terms = returned_result.reshape(capacity, owner_count, model_width)
    own_place = lax.dynamic_index_in_dim(
        placing, lax.axis_index("tensor"), 0, keepdims=False
    ).astype(jnp.float32)
    adapter_rows = jnp.einsum(
        "rjc,cjd->rd", own_place, gathered_terms, precision=lax.Precision.HIGHEST
    )
    return (base_output_rows + 2.0 * adapter_rows).astype(jnp.bfloat16)


def solution(mesh):
    short_line = mesh.shape["adapter"] == 4 and mesh.shape["tensor"] == 4
    return jax.shard_map(
        fused if short_line else per_device,
        mesh=mesh,
        in_specs=(
            P(("group", "adapter"), "tensor"),
            P(("group", "adapter"), None, "tensor"),
            P(("group", "adapter"), None, "tensor"),
            P(("group", "adapter")),
            P(("group", "adapter"), None),
            P("group"),
            P("tensor", "adapter"),
            P(("group", "adapter"), "tensor", None),
            P(("group", "adapter"), None, None),
        ),
        out_specs=P(("group", "adapter", "tensor"), None),
        check_vma=False,
    )
```
